512 devices in a mesh: gen: 64 (over z, y), net: 8 (over x, core).
Axes of the slice: x: 4, y: 4, z: 16, core: 2. Of those that a mesh axis runs over, the one named last changes fastest.
Arguments:
- state: float32 [6, 256, 16384], P(None, 'net', 'gen'), as said below
- params: float32 [13, 16384], P(None, 'gen'), as said below
- gen_count: int32 [64], P('gen'), may hold values from 1 to 256, 12288 in all
- gen_block: int32 [16384, 1], P('gen'), may hold values from 0 to 63; in each aligned block of 256 rows (0 to 255, 256 to 511, ...) at most 6 rows name the same one
- gen_local: int32 [16384], P('gen'), may hold values from 0 to 191
- impedance: bfloat16 [2, 12288, 24576], P(None, 'net', 'gen')
- fault_bus: int32 [256], P('net'), may hold values from 0 to 12287
- cleared: int32 [256], P('net'), may hold values 0 or 1
- fault_volt: float32 [2, 256], P(None, 'net'), may hold values from -0.3 to 0.3
Outputs:
- slope: float32 [6, 256, 16384], P(None, 'net', 'gen')
The draws below stay inside these ranges and needn't reach their ends.
Inputs may be any that keep to these rules, and one draw needn't show every extreme that they name: `gen_block`: among the 256 slots of one gen index, at most 6 name one bus block. Entries lie in the ranges of the state rows: angle within pi, speed deviation within 0.6, emfs and field voltage positive except the d subtransient emf. `params`: reactances satisfy Xd > Xdt > Xs and Xq > Xs; all parameters are positive.
All inputs are finite; a program needn't handle non-finite values. No bound on the sum of `gen_count` or of `cleared` on one device may be relied on, other than what follows from the above.
Results may differ from the reference program's by a relative error of at most 0.00065.
The reference program's roundings to bfloat16 on the way (of `inject`) count: a program that leaves them out, or rounds other values in their place, can miss the bound.
Values may be sent and summed in bfloat16 or wider, within the bound.
A program may use at most 64 MiB of HBM per device.

```python
import math
import jax
import jax.numpy as jnp
import numpy as np

BUS_DEV = 192
GCAP = 256
NB = 12288
NG = 12288
NGS = 16384
SCEN = 256
SUB = 24
IN_DEV = 1536
SEND_CAP = 6
N_GEN = 64
N_NET = 8


def draw_state(key, part):
    key = jax.random.fold_in(key, 11)
    lower = jnp.array([-3.14159, -0.6, 0.8, 0.7, -0.3, 1.0], jnp.float32)
    upper = jnp.array([3.14159, 0.6, 1.3, 1.2, 0.5, 2.5], jnp.float32)
    unit = jax.random.uniform(key, (6, SCEN, NGS), jnp.float32)
    return lower[:, None, None] + (upper - lower)[:, None, None] * unit


def draw_params(key, part):
    key = jax.random.fold_in(key, 12)
    lower = jnp.array([2.0, 0.5, 4.0, 0.2, 0.2, 1.2, 0.45, 0.25, 1.0, 5.0, 0.5, 0.9, 0.5], jnp.float32)
    upper = jnp.array([6.0, 3.0, 8.0, 0.5, 0.5, 2.0, 0.6, 0.4, 1.8, 25.0, 2.0, 1.2, 2.5], jnp.float32)
    unit = jax.random.uniform(key, (13, NGS), jnp.float32)
    return jnp.exp(jnp.log(lower)[:, None] + (jnp.log(upper) - jnp.log(lower))[:, None] * unit)


def draw_impedance(key, part):
    key = jax.random.fold_in(key, 13)
    noise = jax.random.normal(key, (2, NB, 2 * NB), jnp.float32) * (64.0 * NB) ** (-0.5)
    in_index = jnp.arange(NB, dtype=jnp.int32)
    block_net = in_index // IN_DEV
    rest = in_index % IN_DEV
    bus_in = rest // SUB * BUS_DEV + block_net * SUB + rest % SUB
    out_index = jnp.arange(2 * NB, dtype=jnp.int32)
    part_out = out_index % (2 * BUS_DEV) // BUS_DEV
    bus_out = out_index // (2 * BUS_DEV) * BUS_DEV + out_index % BUS_DEV
    same_bus = (bus_in[:, None] == bus_out[None, :]).astype(jnp.float32)
    same_part = (jnp.arange(2, dtype=jnp.int32)[:, None] == part_out[None, :]).astype(jnp.float32)
    diagonal = 0.3 * same_part[:, None, :] * same_bus[None, :, :]
    return (noise + diagonal).astype(jnp.bfloat16)


def touch_ends(drawn, own_key, smallest, top_value):
    longest = drawn.shape.index(max(drawn.shape))
    spots = []
    for shift in (0, 1):
        where = [jax.random.randint(jax.random.fold_in(own_key, axis), (), 0, length) for axis, length in enumerate(drawn.shape)]
        where[longest] = (where[longest] + shift) % drawn.shape[longest]
        spots.append(tuple(where))
    return drawn.at[spots[0]].set(smallest).at[spots[1]].set(top_value)


def block_scale(stream_key, extent, pieces, low, largest):
    level, own = 1.0, jax.random.fold_in(stream_key, 6)
    for axis_at, parts in pieces:
        draws = jnp.exp(jax.random.uniform(jax.random.fold_in(own, axis_at), (parts,), jnp.float32, low / len(pieces), largest / len(pieces)))
        level = level * jnp.repeat(draws, extent[axis_at] // parts).reshape([-1 if axis == axis_at else 1 for axis in range(len(extent))])
    return level


def length_profile(amount, total, most, lean):
    loads = [(1 << 20) // math.isqrt(grade ** lean) + 1 for grade in range(2, amount + 1)]
    spare, given = total - most - (amount - 1), [1] * (amount - 1)
    while spare > 0:
        free = [i for i in range(amount - 1) if given[i] < most]
        pool, budget = sum([loads[i] for i in free]), spare
        for i in free:
            addition = min(most - given[i], max(1, budget * loads[i] // pool), spare)
            given[i] = given[i] + addition
            spare = spare - addition
    return np.array([most] + given)


def uneven_parts(own_key, count, total, bound, lean):
    if count == 2:
        one = jax.random.randint(own_key, (), max(1, total - bound), min(bound, total - 1) + 1)
        return jnp.stack([one, total - one])
    sizes = jnp.asarray(length_profile(count, total, bound, lean), jnp.int32)
    twos = (count - 1) // 2
    source_of, taker = sizes[1:1 + 2 * twos:2], sizes[2:2 + 2 * twos:2]
    slack = jnp.minimum(source_of - 1, bound - taker)
    shifted = jax.random.randint(jax.random.fold_in(own_key, 1), (twos,), 0, 1 << 20) % (slack + 1)
    sizes = sizes.at[1:1 + 2 * twos:2].set(source_of - shifted).at[2:2 + 2 * twos:2].set(taker + shifted)
    return sizes[jax.random.permutation(jax.random.fold_in(own_key, 2), count)]


def shared_out(own_key, own, number, rows, amount, top, bound, lean):
    sequence = jax.random.permutation(own_key, amount)
    heavy_load, ordinary = load_shares(amount, rows * top, bound, lean, True), load_shares(amount, rows * top, bound, lean, False)
    places = jnp.arange(amount)

    def named(lengths, turn):
        used = int((lengths > 0).sum())
        fixed = max(1, used // 4)
        shifted = fixed + (places - fixed + turn * (used - fixed)) % max(1, amount - fixed)
        return jnp.zeros((amount,), jnp.int32).at[sequence[jnp.where(places < fixed, places, shifted)]].set(jnp.asarray(lengths, jnp.int32))

    lengths = jnp.where(number % 4 == 0, named(heavy_load, number // 4), named(ordinary, number - number // 4 - 1))
    mixed = jax.random.permutation(jax.random.fold_in(own, 3), amount)
    donor, taker = mixed[0:amount // 2 * 2:2], mixed[1:amount // 2 * 2:2]
    slack = jnp.minimum(lengths[donor] - 1, bound - lengths[taker]) // 2
    slack = jnp.where((donor == sequence[0]) | (taker == sequence[0]) | (lengths[taker] == 0), 0, jnp.maximum(slack, 0))
    shifted = jax.random.randint(jax.random.fold_in(own, 4), (amount // 2,), 0, 1 << 20) % (slack + 1)
    lengths = lengths.at[donor].add(-shifted).at[taker].add(shifted)
    members = jnp.searchsorted(jnp.cumsum(lengths), jnp.arange(rows * top), side="right").astype(jnp.int32)
    table = members.reshape(top, rows).T
    table = table[jax.random.permutation(jax.random.fold_in(own, 1), rows)]
    turn = jax.random.randint(jax.random.fold_in(own, 2), (rows, 1), 0, top)
    return jnp.take_along_axis(table, (jnp.arange(top)[None, :] + turn) % top, axis=1)


def load_shares(number_of, total, reach, skew, full):
    portions = [(1 << 20) // math.isqrt(rank ** skew) + 1 for rank in range(1, number_of + 1)]
    largest = reach if full else min(reach, max(-(-total // number_of), total * portions[0] // sum(portions)))
    least = 1 if total - largest >= number_of - 1 else 0
    holding, surplus = [largest] + [least] * (number_of - 1), total - largest - least * (number_of - 1)
    while surplus > 0:
        movable = [i for i in range(1, number_of) if holding[i] < largest] or [i for i in range(1, number_of) if holding[i] < reach]
        pool, left = sum([portions[i] for i in movable]), surplus
        for i in movable:
            more = min(reach - holding[i], max(1, left * portions[i] // pool), surplus)
            holding[i] = holding[i] + more
            surplus = surplus - more
    return np.array(holding)


def setup_inputs(seed: int = 0) -> dict:
    streams_of = jax.random.split(jax.random.key(seed), 10)
    state = draw_state(jax.random.fold_in(streams_of[9], 71), 0)
    params = draw_params(jax.random.fold_in(streams_of[9], 71), 0)
    gen_count = uneven_parts(streams_of[2], N_GEN, NG, GCAP, 2).astype(jnp.int32)
    gen_block_keys = jax.random.split(jax.random.fold_in(streams_of[3], 1), NGS // GCAP)
    gen_block_turns = jax.random.permutation(jax.random.fold_in(streams_of[3], 3), NGS // GCAP)
    gen_block = jax.vmap(lambda own, number: shared_out(jax.random.fold_in(streams_of[3], 2), own, number, GCAP, N_GEN, 1, SEND_CAP, 2))(gen_block_keys, gen_block_turns).reshape((NGS, 1))
    gen_local = touch_ends(jax.random.randint(streams_of[4], (NGS,), 0, BUS_DEV), jax.random.fold_in(streams_of[4], 1), 0, BUS_DEV - 1).astype(jnp.int32)
    impedance = draw_impedance(jax.random.fold_in(streams_of[9], 71), 0)
    fault_bus = touch_ends(jax.random.randint(streams_of[6], (SCEN,), 0, NB), jax.random.fold_in(streams_of[6], 1), 0, NB - 1).astype(jnp.int32)
    cleared = touch_ends((jax.random.randint(streams_of[7], (SCEN,), 0, 2) < 1).astype(jnp.int32), jax.random.fold_in(streams_of[7], 1), 0, 1)
    fault_volt = jnp.clip(jax.random.uniform(streams_of[8], (2, SCEN), jnp.float32, -0.3, 0.3) * block_scale(streams_of[8], (2, SCEN), ((1, 8),), -0.4, 0.0), -0.3, 0.3)
    return dict(state=state, params=params, gen_count=gen_count, gen_block=gen_block, gen_local=gen_local, impedance=impedance, fault_bus=fault_bus, cleared=cleared, fault_volt=fault_volt)


def machine_emf(state, params):
    delta, eq_s, ed_s = (state[0], state[3], state[4])
    sin_d = jnp.sin(delta)
    cos_d = jnp.cos(delta)
    emf_re = ed_s * sin_d + eq_s * cos_d
    emf_im = eq_s * sin_d - ed_s * cos_d
    return (sin_d, cos_d, emf_re, emf_im)

def machine_slope(state, params, active, volt_re, volt_im):
    sin_d, cos_d, emf_re, emf_im = machine_emf(state, params)
    omega, eq_t, eq_s, ed_s, efd = (state[1], state[2], state[3], state[4], state[5])
    sub_x = params[7]
    gen_re = (emf_im - volt_im) / sub_x
    gen_im = (volt_re - emf_re) / sub_x
    cur_d = gen_re * sin_d - gen_im * cos_d
    cur_q = gen_re * cos_d + gen_im * sin_d
    power = ed_s * cur_d + eq_s * cur_q
    term = jnp.sqrt(volt_re * volt_re + volt_im * volt_im + 0.01)
    first = omega
    second = (params[12] - power - params[1] * omega) / (2.0 * params[0])
    third = (efd - eq_t - (params[5] - params[6]) * cur_d) / params[2]
    fourth = (eq_t - eq_s - (params[6] - sub_x) * cur_d) / params[3]
    fifth = ((params[8] - sub_x) * cur_q - ed_s) / params[4]
    sixth = (params[9] * (params[11] - term) - efd) / params[10]
    return jnp.stack([first, second, third, fourth, fifth, sixth]) * active

def reference(state, params, gen_count, gen_block, gen_local, impedance, fault_bus, cleared, fault_volt):
    num_slots = state.shape[2]
    num_scen = state.shape[1]
    slot_ids = jnp.arange(num_slots, dtype=jnp.int32)
    counts = gen_count[slot_ids // GCAP]
    active = (slot_ids % GCAP < counts).astype(jnp.float32)
    bus_of = gen_block[:, 0] * BUS_DEV + gen_local
    sin_d, cos_d, emf_re, emf_im = machine_emf(state, params)
    sub_x = params[7]
    norton = jnp.stack([emf_im / sub_x, -emf_re / sub_x]) * active
    inject = jnp.stack([jax.ops.segment_sum(norton[0].T, bus_of, num_segments=NB), jax.ops.segment_sum(norton[1].T, bus_of, num_segments=NB)])
    hit = (jnp.arange(NB, dtype=jnp.int32)[:, None] == fault_bus[None, :]).astype(jnp.float32)
    hit = hit * (1 - cleared).astype(jnp.float32)[None, :]
    inject = inject - 10.0 * fault_volt[:, None, :] * hit[None]
    inject = inject.astype(jnp.bfloat16)
    ordered = inject.reshape(2, N_GEN, N_NET, SUB, num_scen).transpose(4, 0, 2, 1, 3).reshape(num_scen, 2 * NB)
    volts = jnp.dot(ordered, impedance.reshape(2 * NB, 2 * NB), preferred_element_type=jnp.float32)
    volts = volts.reshape(num_scen, N_GEN, 2, BUS_DEV).transpose(0, 2, 1, 3).reshape(num_scen, 2, NB)
    at_gen = jnp.take(volts, bus_of, axis=2)
    return machine_slope(state, params, active, at_gen[:, 0], at_gen[:, 1])
```

```python
import functools

import jax
import jax.numpy as jnp
from jax import lax
from jax.experimental import pallas as pl
from jax.experimental.pallas import tpu as pltpu
from jax.sharding import PartitionSpec as P

F32 = jnp.float32
BF16 = jnp.bfloat16
NZ, NY, NX, NCORE = 16, 4, 4, 2
NGEN, NNET = NZ * NY, NX * NCORE
SCN = 32
SLOTS = 256
BUS = 192
SUB = BUS // NNET
CAP = 6
HALF = NZ // 2
NT = (((1,), (1,)), ((), ()))


def remote(src, dst, send_sem, recv_sem, gen, net):
    return pltpu.make_async_remote_copy(
        src_ref=src,
        dst_ref=dst,
        send_sem=send_sem,
        recv_sem=recv_sem,
        device_id=(gen, net),
        device_id_type=pl.DeviceIdType.MESH,
    )


def three(v):
    hi = v.astype(BF16)
    rest = v - hi.astype(F32)
    mid = rest.astype(BF16)
    lo = (rest - mid.astype(F32)).astype(BF16)
    return hi, mid, lo


def lane_iota(shape):
    return lax.broadcasted_iota(jnp.int32, shape, len(shape) - 1)


def row_iota(shape):
    return lax.broadcasted_iota(jnp.int32, shape, 0)


def pack(hot, vals):
    hi, mid, lo = three(vals)
    rhs = jnp.concatenate([hi, mid, lo, lo], axis=0)
    out = lax.dot_general(hot, rhs, NT, preferred_element_type=F32)
    left, right = out[:, :128], out[:, 128:]
    both = left + pltpu.roll(left, 64, 1) + right
    low = lane_iota((NGEN, 128)) < 64
    rows = []
    for j in range(CAP // 2):
        even = both[2 * j * NGEN : (2 * j + 1) * NGEN]
        odd = both[(2 * j + 1) * NGEN : (2 * j + 2) * NGEN]
        rows.append(jnp.where(low, even, odd))
    return rows


def unpack(hot, rows):
    every = jnp.concatenate(rows, axis=0)
    turned = pltpu.roll(every, 64, 1)
    low = lane_iota(every.shape) < 64
    vals = jnp.concatenate([jnp.where(low, every, turned), jnp.where(low, turned, every)], axis=0)
    hi, mid, lo = three(vals)
    first = jnp.where(lane_iota(vals.shape) < 64, hi.astype(F32), mid.astype(F32)).astype(BF16)
    rhs = jnp.concatenate([first, lo], axis=1)
    out = jnp.dot(hot, rhs, preferred_element_type=F32)
    left, right = out[:, :128], out[:, 128:]
    return left + pltpu.roll(left, 64, 1) + right


def kernel(
    state,
    params,
    count,
    block,
    local,
    z_hbm,
    fbus,
    cleared,
    fvolt,
    out,
    zbuf,
    zt,
    gath,
    sbox,
    rbox,
    smsg,
    rmsg,
    vbuf,
    cbuf,
    wbuf,
    xbuf,
    sback,
    rback,
    keep,
    z_sem,
    box_s,
    box_r,
    msg_s,
    msg_r,
    yi_s,
    yi_r,
    zz_s,
    zz_r,
    zy_s,
    zy_r,
    ys_s,
    ys_r,
    yr_s,
    yr_r,
    core_s,
    core_r,
    x_s,
    x_r,
    back_s,
    back_r,
):
    g = lax.axis_index("gen")
    n = lax.axis_index("net")
    z, y = g // NY, g % NY
    x, c = n // NCORE, n % NCORE
    barrier = pltpu.get_barrier_semaphore()

    def greet_gen(i, carry):
        pl.semaphore_signal(
            barrier, inc=1, device_id=((g + i) % NGEN, n), device_id_type=pl.DeviceIdType.MESH
        )
        return carry

    def greet_net(i, carry):
        pl.semaphore_signal(
            barrier, inc=1, device_id=(g, (n + i) % NNET), device_id_type=pl.DeviceIdType.MESH
        )
        return carry

    lax.fori_loop(1, NGEN, greet_gen, 0)
    lax.fori_loop(1, NNET, greet_net, 0)
    z_copy = pltpu.make_async_copy(z_hbm, zbuf, z_sem)
    z_copy.start()

    tgt_s = block[...]
    ii, jj = row_iota((SLOTS, SLOTS)), lane_iota((SLOTS, SLOTS))
    tgt_b = jnp.broadcast_to(tgt_s, (SLOTS, SLOTS)).astype(F32)
    tgt_l = jnp.sum(jnp.where(ii == jj, tgt_b, 0.0), axis=0, keepdims=True)
    same = tgt_b == tgt_l
    rank_l = jnp.sum(jnp.where(same & (ii < jj), 1.0, 0.0), axis=0, keepdims=True)
    rank_s = jnp.sum(jnp.where(same & (jj < ii), 1.0, 0.0), axis=1, keepdims=True).astype(jnp.int32)
    code_l = rank_l * NGEN + tgt_l
    code_s = (rank_s % 2) * (3 * NGEN) + (rank_s // 2) * NGEN + tgt_s
    send_hot = jnp.where(
        row_iota((CAP * NGEN, SLOTS)).astype(F32) == code_l, 1.0, 0.0
    ).astype(BF16)

    active = (lane_iota((1, SLOTS)) < count[0]).astype(F32)
    delta, eq_s, ed_s = state[0], state[3], state[4]
    sin_d = jnp.sin(delta)
    cos_d = jnp.cos(delta)
    emf_re = ed_s * sin_d + eq_s * cos_d
    emf_im = eq_s * sin_d - ed_s * cos_d
    keep[0] = sin_d
    keep[1] = cos_d
    keep[2] = emf_re
    keep[3] = emf_im
    sub_x = params[7:8, :]
    cur = jnp.concatenate([emf_im / sub_x * active, -emf_re / sub_x * active], axis=0)
    for j, row in enumerate(pack(send_hot, cur)):
        sbox[:, j, :] = row
    ids = lax.dot_general(
        send_hot,
        jnp.broadcast_to((local[...] + 1).astype(F32), (128, SLOTS)).astype(BF16),
        NT,
        preferred_element_type=F32,
    )
    lane = lane_iota((NGEN, 128))
    id_row = jnp.zeros((NGEN, 128), F32)
    for r in range(CAP):
        id_row = jnp.where(lane == r, ids[r * NGEN : (r + 1) * NGEN], id_row)
    sbox[:, 3, :] = id_row

    pl.semaphore_wait(barrier, NGEN - 1 + NNET - 1)

    def send_box(i, carry):
        peer = (g + i) % NGEN
        remote(sbox.at[peer], rbox.at[g], box_s, box_r, peer, n).start()
        return carry

    lax.fori_loop(1, NGEN, send_box, 0)
    rbox[g] = sbox[g]
    z_copy.wait()

    def turn(j):
        parts = [zbuf[p, j].astype(F32) for p in range(2)]
        rows = []
        for k in range(8):
            a = k * SUB
            rows += [
                parts[0][a : a + 16],
                parts[1][a : a + 16],
                parts[0][a + 16 : a + 24],
                parts[1][a + 16 : a + 24],
            ]
        zt[j] = jnp.concatenate(rows, axis=0).T.astype(BF16)

    all_boxes = remote(
        sbox.at[pl.ds(0, NGEN - 1)], rbox.at[pl.ds(0, NGEN - 1)], box_s, box_r, g, n
    )
    all_boxes.wait_recv()

    ids_in = rbox[:, 3, :]
    ids_t = ids_in.T
    id_lane = jnp.concatenate([ids_t[r : r + 1] for r in (0, 2, 4, 1, 3, 5)], axis=1)
    row = row_iota((256, 1))
    part, i16 = (row % 128) // 16, row % 16
    bus = part * SUB + jnp.where(row < 128, i16, 16 + i16 % 8)
    bus_hot = jnp.where((bus + 1).astype(F32) == id_lane, 1.0, 0.0).astype(BF16)
    summed = unpack(bus_hot, [rbox[:, j, :] for j in range(3)])
    fb, cl = fbus[...], cleared[...]
    fb4 = jnp.concatenate([fb] * 4, axis=1)
    on4 = 1.0 - jnp.concatenate([cl] * 4, axis=1).astype(F32)
    fv4 = jnp.concatenate([fvolt[0:1], fvolt[1:2]] * 2, axis=1)
    hit = jnp.where(bus + g * BUS == fb4, 1.0, 0.0) * on4
    inject = summed - 10.0 * fv4 * hit
    first, second = inject[:128], inject[128:]
    i16 = row_iota((128, 128)) % 16
    second = jnp.where(i16 < 8, second, pltpu.roll(second, 96, 1))
    message = jnp.where(lane_iota((128, 128)) < 64, first, second).astype(BF16)
    smsg[...] = message.reshape(NNET, 16, 128)

    def send_msg(i, carry):
        peer = (n + i) % NNET
        remote(smsg.at[peer], rmsg.at[n], msg_s, msg_r, g, peer).start()
        return carry

    lax.fori_loop(1, NNET, send_msg, 0)
    rmsg[n] = smsg[n]
    all_msgs = remote(
        smsg.at[pl.ds(0, NNET - 1)], rmsg.at[pl.ds(0, NNET - 1)], msg_s, msg_r, g, n
    )
    all_msgs.wait_recv()
    tiles = [rmsg[k].astype(F32) for k in range(NNET)]
    for j in range(3):
        chunk = jnp.concatenate([t[:, SCN * j : SCN * (j + 1)] for t in tiles], axis=1)
        gath[z, y, j] = chunk.astype(BF16)

    yp, ym = (y + 1) % NY, (y + NY - 1) % NY
    zp, zm = (z + 1) % NZ, (z + NZ - 1) % NZ
    right, left = z * NY + yp, z * NY + ym
    up, down = zp * NY + y, zm * NY + y

    def own(slot):
        return gath.at[slot, y, pl.ds(1, 2)]

    def own_copy(slot, way, t):
        return remote(own(slot), own(slot), zz_s.at[way, t], zz_r.at[way, t], up if way == 0 else down, n)

    def bundle_copy(slot, piece, way, t):
        ref = gath.at[slot, pl.ds(2 * piece, 2), 0]
        return remote(
            ref, ref, zy_s.at[way, piece, t], zy_r.at[way, piece, t], up if way == 0 else down, n
        )

    def side_copy(slot, way, k, arriving=False):
        col = (ym if way == 0 else yp) if arriving else y
        ref = gath.at[slot, col, pl.ds(1, 2)]
        return remote(ref, ref, ys_s.at[way, k], ys_r.at[way, k], right if way == 0 else left, n)

    def relay_copy(slot, way, k, arriving=False):
        if arriving:
            col = (y + 2) % NY
        else:
            col = ym if way == 0 else yp
        ref = gath.at[slot, col, 1 + way]
        return remote(ref, ref, yr_s.at[way, k], yr_r.at[way, k], right if way == 0 else left, n)

    for d in range(1, NY):
        ref = gath.at[z, y, 0]
        remote(ref, ref, yi_s, yi_r, z * NY + (y + d) % NY, n).start()
    for way in range(2):
        own_copy(z, way, 0).start()
    for way in range(2):
        side_copy(z, way, 0).start()
    ref = gath.at[z, pl.ds(0, NY - 1), 0]
    y_first = remote(ref, ref, yi_s, yi_r, g, n)
    y_first.wait_recv()
    for piece in range(2):
        for way in range(2):
            bundle_copy(z, piece, way, 0).start()

    def slot_at(k):
        return (z + NZ - (k + 1) // 2) % NZ if k % 2 else (z + k // 2) % NZ

    relayed = []
    for t in range(1, HALF + 1):
        ways = (0, 1) if t < HALF else (0,)
        slots = (slot_at(2 * t - 1), slot_at(2 * t))
        for way in ways:
            own_copy(slots[way], way, t - 1).wait_recv()
            if t < HALF - way:
                own_copy(slots[way], way, t).start()
        for way in ways:
            for side in range(2):
                side_copy(slots[way], side, 2 * t - 1 + way).start()
        for piece in range(2):
            for way in ways:
                bundle_copy(slots[way], piece, way, t - 1).wait_recv()
                if t < HALF - way:
                    bundle_copy(slots[way], piece, way, t).start()
        ready = [0] if t == 1 else [2 * t - 3, 2 * t - 2]
        for k in ready:
            for side in range(2):
                side_copy(slot_at(k), side, k, arriving=True).wait_recv()
                relay_copy(slot_at(k), side, k).start()
        turn(t - 1)
    last = NZ - 1
    for side in range(2):
        side_copy(slot_at(last), side, last, arriving=True).wait_recv()
        relay_copy(slot_at(last), side, last).start()
    for k in range(NZ):
        for side in range(2):
            relay_copy(slot_at(k), side, k, arriving=True).wait_recv()

    acc = jnp.zeros((2 * BUS, NNET * SCN), F32)
    for j in range(NZ // 2):
        rows = gath[2 * j : 2 * j + 2].reshape(2 * BUS, NNET * SCN)
        acc = acc + jnp.dot(zt[j], rows, preferred_element_type=F32)
    vbuf[...] = acc.T.reshape(NX, NCORE, SCN, 2 * BUS)

    sib = n + 1 - 2 * c
    core_copy = remote(vbuf.at[:, 1 - c], cbuf, core_s, core_r, g, sib)
    core_copy.start()
    core_copy.wait_recv()
    wbuf[...] = vbuf[:, c] + cbuf[...]
    for d in range(1, NX):
        peer = (x + d) % NX
        remote(wbuf.at[peer], xbuf.at[x], x_s, x_r, g, peer * NCORE + c).start()
    xbuf[x] = wbuf[x]
    x_all = remote(wbuf.at[pl.ds(0, NX - 1)], xbuf.at[pl.ds(0, NX - 1)], x_s, x_r, g, n)
    x_all.wait_recv()
    volts = (xbuf[0] + xbuf[1]) + (xbuf[2] + xbuf[3])

    bus_lane = lane_iota((NGEN, BUS)) + 1
    back_hot = jnp.concatenate(
        [
            jnp.where(ids_in[:, r : r + 1].astype(jnp.int32) == bus_lane, 1.0, 0.0)
            for r in range(CAP)
        ],
        axis=0,
    ).astype(BF16)
    both = jnp.concatenate([volts[:, :BUS], volts[:, BUS:]], axis=0)
    for j, row in enumerate(pack(back_hot, both)):
        sback[:, j, :] = row
    sback[:, 3, :] = jnp.zeros((NGEN, 128), F32)

    def send_back(i, carry):
        peer = (g + i) % NGEN
        remote(sback.at[peer], rback.at[g], back_s, back_r, peer, n).start()
        return carry

    lax.fori_loop(1, NGEN, send_back, 0)
    rback[g] = sback[g]
    slot_hot = jnp.where(lane_iota((SLOTS, CAP * NGEN)) == code_s, 1.0, 0.0).astype(BF16)
    all_back = remote(
        sback.at[pl.ds(0, NGEN - 1)], rback.at[pl.ds(0, NGEN - 1)], back_s, back_r, g, n
    )
    all_back.wait_recv()
    at_gen = unpack(slot_hot, [rback[:, j, :] for j in range(3)]).T
    v_re, v_im = at_gen[:SCN], at_gen[SCN : 2 * SCN]

    sin_d, cos_d, emf_re, emf_im = keep[0], keep[1], keep[2], keep[3]
    omega, eq_t, eq_s, ed_s, efd = state[1], state[2], state[3], state[4], state[5]
    par = [params[k : k + 1, :] for k in range(13)]
    gen_re = (emf_im - v_im) / sub_x
    gen_im = (v_re - emf_re) / sub_x
    cur_d = gen_re * sin_d - gen_im * cos_d
    cur_q = gen_re * cos_d + gen_im * sin_d
    power = ed_s * cur_d + eq_s * cur_q
    term = jnp.sqrt(v_re * v_re + v_im * v_im + 0.01)
    out[0] = omega * active
    out[1] = (par[12] - power - par[1] * omega) / (2.0 * par[0]) * active
    out[2] = (efd - eq_t - (par[5] - par[6]) * cur_d) / par[2] * active
    out[3] = (eq_t - eq_s - (par[6] - sub_x) * cur_d) / par[3] * active
    out[4] = ((par[8] - sub_x) * cur_q - ed_s) / par[4] * active
    out[5] = (par[9] * (par[11] - term) - efd) / par[10] * active

    all_boxes.wait_send()
    all_msgs.wait_send()
    y_first.wait_send()
    for k in range(NZ):
        for side in range(2):
            side_copy(slot_at(k), side, k).wait_send()
            relay_copy(slot_at(k), side, k).wait_send()
    for t in range(HALF):
        for way in range(2):
            if t < HALF - way:
                own_copy(z, way, t).wait_send()
                for piece in range(2):
                    bundle_copy(z, piece, way, t).wait_send()
    core_copy.wait_send()
    x_all.wait_send()
    all_back.wait_send()


def body(state, params, gen_count, gen_block, gen_local, impedance, fault_bus, cleared, fault_volt):
    vmem = pl.BlockSpec(memory_space=pltpu.VMEM)
    dma = pltpu.SemaphoreType.DMA
    return pl.pallas_call(
        kernel,
        out_shape=jax.ShapeDtypeStruct(state.shape, F32),
        in_specs=[
            vmem,
            vmem,
            pl.BlockSpec(memory_space=pltpu.SMEM),
            vmem,
            vmem,
            pl.BlockSpec(memory_space=pl.ANY),
            vmem,
            vmem,
            vmem,
        ],
        out_specs=vmem,
        scratch_shapes=[
            pltpu.VMEM((2, NZ // 2, BUS, 2 * BUS), BF16),
            pltpu.VMEM((NZ // 2, 2 * BUS, 2 * BUS), BF16),
            pltpu.VMEM((NZ, NY, 3, 16, NNET * SCN), BF16),
            pltpu.VMEM((NGEN, 4, 128), F32),
            pltpu.VMEM((NGEN, 4, 128), F32),
            pltpu.VMEM((NNET, 16, 128), BF16),
            pltpu.VMEM((NNET, 16, 128), BF16),
            pltpu.VMEM((NX, NCORE, SCN, 2 * BUS), F32),
            pltpu.VMEM((NX, SCN, 2 * BUS), F32),
            pltpu.VMEM((NX, SCN, 2 * BUS), F32),
            pltpu.VMEM((NX, SCN, 2 * BUS), F32),
            pltpu.VMEM((NGEN, 4, 128), F32),
            pltpu.VMEM((NGEN, 4, 128), F32),
            pltpu.VMEM((4, SCN, SLOTS), F32),
            dma,
            dma,
            dma,
            dma,
            dma,
            dma,
            dma,
            dma((2, HALF)),
            dma((2, HALF)),
            dma((2, 2, HALF)),
            dma((2, 2, HALF)),
            dma((2, NZ)),
            dma((2, NZ)),
            dma((2, NZ)),
            dma((2, NZ)),
            dma,
            dma,
            dma,
            dma,
            dma,
            dma,
        ],
        compiler_params=pltpu.CompilerParams(
            collective_id=0, has_side_effects=True, vmem_limit_bytes=40 * 1024 * 1024
        ),
    )(
        state,
        params,
        gen_count,
        gen_block,
        gen_local.reshape(1, SLOTS),
        impedance.reshape(2, NZ // 2, BUS, 2 * BUS),
        fault_bus.reshape(1, SCN),
        cleared.reshape(1, SCN),
        fault_volt,
    )


def solution(mesh):
    in_specs = (
        P(None, "net", "gen"),
        P(None, "gen"),
        P("gen"),
        P("gen", None),
        P("gen"),
        P(None, "net", "gen"),
        P("net"),
        P("net"),
        P(None, "net"),
    )
    return jax.shard_map(
        body, mesh=mesh, in_specs=in_specs, out_specs=P(None, "net", "gen"), check_vma=False
    )
```

```python
import functools

import jax
import jax.numpy as jnp
from jax import lax
from jax.experimental import pallas as pl
from jax.experimental.pallas import tpu as pltpu
from jax.sharding import PartitionSpec as P

F32 = jnp.float32
BF16 = jnp.bfloat16
NZ, NY, NX, NCORE = 16, 4, 4, 2
NGEN, NNET = NZ * NY, NX * NCORE
SCN = 32
SLOTS = 256
BUS = 192
SUB = BUS // NNET
CAP = 6
FAR = (0, NZ // 4, 3 * NZ // 4, NZ // 2)
BACK = (0, 2, 1, 3)
NT = (((1,), (1,)), ((), ()))


def remote(src, dst, send_sem, recv_sem, gen, net):
    return pltpu.make_async_remote_copy(
        src_ref=src,
        dst_ref=dst,
        send_sem=send_sem,
        recv_sem=recv_sem,
        device_id=(gen, net),
        device_id_type=pl.DeviceIdType.MESH,
    )


def three(v):
    hi = v.astype(BF16)
    rest = v - hi.astype(F32)
    mid = rest.astype(BF16)
    lo = (rest - mid.astype(F32)).astype(BF16)
    return hi, mid, lo


def lane_iota(shape):
    return lax.broadcasted_iota(jnp.int32, shape, len(shape) - 1)


def row_iota(shape):
    return lax.broadcasted_iota(jnp.int32, shape, 0)


def pack(hot, vals):
    hi, mid, lo = three(vals)
    rhs = jnp.concatenate([hi, mid, lo, lo], axis=0)
    out = lax.dot_general(hot, rhs, NT, preferred_element_type=F32)
    left, right = out[:, :128], out[:, 128:]
    both = left + pltpu.roll(left, 64, 1) + right
    low = lane_iota((NGEN, 128)) < 64
    rows = []
    for j in range(CAP // 2):
        even = both[2 * j * NGEN : (2 * j + 1) * NGEN]
        odd = both[(2 * j + 1) * NGEN : (2 * j + 2) * NGEN]
        rows.append(jnp.where(low, even, odd))
    return rows


def unpack(hot, rows):
    every = jnp.concatenate(rows, axis=0)
    turned = pltpu.roll(every, 64, 1)
    low = lane_iota(every.shape) < 64
    vals = jnp.concatenate([jnp.where(low, every, turned), jnp.where(low, turned, every)], axis=0)
    hi, mid, lo = three(vals)
    first = jnp.where(lane_iota(vals.shape) < 64, hi.astype(F32), mid.astype(F32)).astype(BF16)
    rhs = jnp.concatenate([first, lo], axis=1)
    out = jnp.dot(hot, rhs, preferred_element_type=F32)
    left, right = out[:, :128], out[:, 128:]
    return left + pltpu.roll(left, 64, 1) + right


def kernel(
    state_h,
    params_h,
    count_h,
    block_h,
    local_h,
    z_hbm,
    fbus_h,
    cleared_h,
    fvolt_h,
    out,
    state,
    params,
    count,
    block,
    local,
    zbuf,
    fbus,
    cleared,
    fvolt,
    zt,
    gath,
    sbox,
    rbox,
    smsg,
    rmsg,
    vbuf,
    cbuf,
    wbuf,
    xbuf,
    sback,
    rback,
    keep,
    back_hot,
    slot_hot,
    in_sem,
    box_s,
    box_r,
    msg_s,
    msg_r,
    near_s,
    near_r,
    side_s,
    side_r,
    core_s,
    core_r,
    x_s,
    x_r,
    back_s,
    back_r,
):
    g = lax.axis_index("gen")
    n = lax.axis_index("net")
    z, y = g // NY, g % NY
    x, c = n // NCORE, n % NCORE
    barrier = pltpu.get_barrier_semaphore()

    def peer_at(i):
        zi, yi = i // NY, i % NY
        dz = NZ + NZ // 2 + ((zi + 1) // 2) * (2 * (zi % 2) - 1)
        dy = 2 + yi + yi // 2 + 2 * (yi // 3)
        return ((z + dz) % NZ) * NY + (y + dy) % NY

    def greet(gen, net):
        pl.semaphore_signal(
            barrier, inc=1, device_id=(gen, net), device_id_type=pl.DeviceIdType.MESH
        )

    def greet_gen(i, carry):
        greet(peer_at(i), n)
        return carry

    lax.fori_loop(0, NGEN - 1, greet_gen, 0)
    for k in (3, 2, 1, 0):

        def greet_net(i, carry, far=FAR[k]):
            greet(((z + far) % NZ) * NY + y, (n + i) % NNET)
            return carry

        lax.fori_loop(1, NNET, greet_net, 0)

    loads = [
        pltpu.make_async_copy(src, dst, in_sem.at[i])
        for i, (src, dst) in enumerate(
            [
                (block_h, block),
                (state_h, state),
                (params_h, params),
                (count_h, count),
                (local_h, local),
                (fbus_h, fbus),
                (cleared_h, cleared),
                (fvolt_h, fvolt),
                (z_hbm, zbuf),
            ]
        )
    ]
    for load in loads:
        load.start()

    loads[0].wait()
    tgt_l = block[...].astype(F32)
    ii, jj = row_iota((SLOTS, SLOTS)), lane_iota((SLOTS, SLOTS))
    same = jnp.broadcast_to(tgt_l, (SLOTS, SLOTS)).T == tgt_l
    rank_l = jnp.sum(jnp.where(same & (ii < jj), 1.0, 0.0), axis=0, keepdims=True)
    send_hot = jnp.where(
        row_iota((CAP * NGEN, SLOTS)).astype(F32) == rank_l * NGEN + tgt_l, 1.0, 0.0
    ).astype(BF16)
    for load in loads[1:8]:
        load.wait()

    active = (lane_iota((1, SLOTS)) < count[0]).astype(F32)
    delta, eq_s, ed_s = state[0], state[3], state[4]
    sin_d = jnp.sin(delta)
    cos_d = jnp.cos(delta)
    emf_re = ed_s * sin_d + eq_s * cos_d
    emf_im = eq_s * sin_d - ed_s * cos_d
    keep[0] = sin_d
    keep[1] = cos_d
    keep[2] = emf_re
    keep[3] = emf_im
    sub_x = params[7:8, :]
    cur = jnp.concatenate([emf_im / sub_x * active, -emf_re / sub_x * active], axis=0)
    for j, row in enumerate(pack(send_hot, cur)):
        sbox[:, j, :] = row
    ids = lax.dot_general(
        send_hot,
        jnp.broadcast_to((local[...] + 1).astype(F32), (128, SLOTS)).astype(BF16),
        NT,
        preferred_element_type=F32,
    )
    lane = lane_iota((NGEN, 128))
    id_row = jnp.zeros((NGEN, 128), F32)
    for r in range(CAP):
        id_row = jnp.where(lane == r, ids[r * NGEN : (r + 1) * NGEN], id_row)
    sbox[:, 3, :] = id_row

    pl.semaphore_wait(barrier, NGEN - 1 + len(FAR) * (NNET - 1))

    def send_box(i, carry):
        peer = peer_at(i)
        remote(sbox.at[peer], rbox.at[g], box_s, box_r, peer, n).start()
        return carry

    lax.fori_loop(0, NGEN - 1, send_box, 0)
    rbox[g] = sbox[g]
    loads[8].wait()

    def turn(j):
        parts = [zbuf[p, j].astype(F32) for p in range(2)]
        rows = []
        for k in range(8):
            a = k * SUB
            rows += [
                parts[0][a : a + 16],
                parts[1][a : a + 16],
                parts[0][a + 16 : a + 24],
                parts[1][a + 16 : a + 24],
            ]
        zt[j] = jnp.concatenate(rows, axis=0).T.astype(BF16)

    for j in range(5):
        turn(j)
    half = (rank_l.astype(jnp.int32) % 2) * (3 * NGEN) + (rank_l.astype(jnp.int32) // 2) * NGEN
    code = half.astype(F32) + tgt_l
    code_s = jnp.broadcast_to(code, (128, SLOTS)).T
    slot_hot[...] = jnp.concatenate(
        [
            jnp.where((lane_iota((SLOTS, 128)) + 128 * k).astype(F32) == code_s, 1.0, 0.0)
            for k in range(3)
        ],
        axis=1,
    ).astype(BF16)
    row = row_iota((256, 1))
    part, i16 = (row % 128) // 16, row % 16
    bus = part * SUB + jnp.where(row < 128, i16, 16 + i16 % 8)
    fb, cl = fbus[...], cleared[...]
    fb4 = jnp.concatenate([fb] * 4, axis=1)
    on4 = 1.0 - jnp.concatenate([cl] * 4, axis=1).astype(F32)
    fv4 = jnp.concatenate([fvolt[0:1], fvolt[1:2]] * 2, axis=1)
    fault = 10.0 * fv4 * (jnp.where(bus + g * BUS == fb4, 1.0, 0.0) * on4)

    all_boxes = remote(
        sbox.at[pl.ds(0, NGEN - 1)], rbox.at[pl.ds(0, NGEN - 1)], box_s, box_r, g, n
    )
    all_boxes.wait_recv()

    ids_in = rbox[:, 3, :]
    ids_t = ids_in.T
    id_lane = jnp.concatenate([ids_t[r : r + 1] for r in (0, 2, 4, 1, 3, 5)], axis=1)
    bus_hot = jnp.where((bus + 1).astype(F32) == id_lane, 1.0, 0.0).astype(BF16)
    summed = unpack(bus_hot, [rbox[:, j, :] for j in range(3)])
    inject = summed - fault
    first, second = inject[:128], inject[128:]
    i16 = row_iota((128, 128)) % 16
    second = jnp.where(i16 < 8, second, pltpu.roll(second, 96, 1))
    message = jnp.where(lane_iota((128, 128)) < 64, first, second).astype(BF16)
    smsg[...] = message.reshape(NNET, 16, 128)

    for k in (3, 1, 2, 0):

        def send_msg(i, carry, k=k):
            peer = (n + i) % NNET
            gen = ((z + FAR[k]) % NZ) * NY + y
            remote(smsg.at[peer], rmsg.at[BACK[k], n], msg_s.at[k], msg_r.at[BACK[k]], gen, peer).start()
            return carry

        lax.fori_loop(0 if k else 1, NNET, send_msg, 0)
    rmsg[0, n] = smsg[n]

    def all_msgs(k):
        count = NNET if k else NNET - 1
        return remote(
            smsg.at[pl.ds(0, count)], rmsg.at[k, pl.ds(0, count)], msg_s.at[k], msg_r.at[k], g, n
        )

    near = (1, NZ - 1, 2)
    side = (1, NY - 1, 2)

    def near_copy(k, way):
        ref = gath.at[(z + FAR[k]) % NZ, y]
        return remote(
            ref, ref, near_s.at[way, k], near_r.at[way, k], ((z + near[way]) % NZ) * NY + y, n
        )

    def send_sides(slot):
        for d in side:
            ref = gath.at[slot, y]
            remote(ref, ref, side_s, side_r, z * NY + (y + d) % NY, n).start()

    def assemble(k):
        slot = (z + FAR[k]) % NZ
        all_msgs(k).wait_recv()
        tiles = [rmsg[k, m].astype(F32) for m in range(NNET)]
        for j in range(3):
            chunk = jnp.concatenate([t[:, SCN * j : SCN * (j + 1)] for t in tiles], axis=1)
            gath[slot, y, j] = chunk.astype(BF16)
        for way in (2, 0, 1):
            near_copy(k, way).start()
        send_sides(slot)

    def arrive(k):
        for way in range(3):
            near_copy(k, way).wait_recv()
            send_sides((z + FAR[k] + NZ - near[way]) % NZ)

    assemble(0)
    turn(5)
    assemble(1)
    assemble(2)
    turn(6)
    arrive(0)
    assemble(3)
    turn(7)
    bus_lane = lane_iota((NGEN, BUS)) + 1
    back_hot[...] = jnp.concatenate(
        [
            jnp.where(ids_in[:, r : r + 1].astype(jnp.int32) == bus_lane, 1.0, 0.0)
            for r in range(CAP)
        ],
        axis=0,
    ).astype(BF16)
    arrive(1)
    arrive(2)
    arrive(3)
    ref = gath.at[pl.ds(0, 3 * NZ // 4)]
    all_sides = remote(ref, ref, side_s, side_r, g, n)
    all_sides.wait_recv()

    acc = jnp.zeros((2 * BUS, NNET * SCN), F32)
    for j in range(NZ // 2):
        rows = gath[2 * j : 2 * j + 2].reshape(2 * BUS, NNET * SCN)
        acc = acc + jnp.dot(zt[j], rows, preferred_element_type=F32)
    vbuf[...] = acc.T.reshape(NX, NCORE, SCN, 2 * BUS)

    sib = n + 1 - 2 * c
    core_copy = remote(vbuf.at[:, 1 - c], cbuf, core_s, core_r, g, sib)
    core_copy.start()
    core_copy.wait_recv()
    wbuf[...] = vbuf[:, c] + cbuf[...]
    for d in (2, 1, 3):
        peer = (x + d) % NX
        remote(wbuf.at[peer], xbuf.at[x], x_s, x_r, g, peer * NCORE + c).start()
    xbuf[x] = wbuf[x]
    x_all = remote(wbuf.at[pl.ds(0, NX - 1)], xbuf.at[pl.ds(0, NX - 1)], x_s, x_r, g, n)
    x_all.wait_recv()
    volts = (xbuf[0] + xbuf[1]) + (xbuf[2] + xbuf[3])

    both = jnp.concatenate([volts[:, :BUS], volts[:, BUS:]], axis=0)
    for j, row in enumerate(pack(back_hot[...], both)):
        sback[:, j, :] = row

    def send_back(i, carry):
        peer = peer_at(i)
        remote(
            sback.at[peer, pl.ds(0, 3)], rback.at[g, pl.ds(0, 3)], back_s, back_r, peer, n
        ).start()
        return carry

    lax.fori_loop(0, NGEN - 1, send_back, 0)
    rback[g, 0:3] = sback[g, 0:3]

    all_boxes.wait_send()
    for k in range(4):
        all_msgs(k).wait_send()
        for way in range(3):
            near_copy(k, way).wait_send()
    all_sides.wait_send()
    core_copy.wait_send()
    x_all.wait_send()

    all_back = remote(
        sback.at[pl.ds(0, NGEN - 1), pl.ds(0, 3)],
        rback.at[pl.ds(0, NGEN - 1), pl.ds(0, 3)],
        back_s,
        back_r,
        g,
        n,
    )
    all_back.wait_recv()
    at_gen = unpack(slot_hot[...], [rback[:, j, :] for j in range(3)]).T
    v_re, v_im = at_gen[:SCN], at_gen[SCN : 2 * SCN]

    sin_d, cos_d, emf_re, emf_im = keep[0], keep[1], keep[2], keep[3]
    omega, eq_t, eq_s, ed_s, efd = state[1], state[2], state[3], state[4], state[5]
    par = [params[k : k + 1, :] for k in range(13)]
    gen_re = (emf_im - v_im) / sub_x
    gen_im = (v_re - emf_re) / sub_x
    cur_d = gen_re * sin_d - gen_im * cos_d
    cur_q = gen_re * cos_d + gen_im * sin_d
    power = ed_s * cur_d + eq_s * cur_q
    term = jnp.sqrt(v_re * v_re + v_im * v_im + 0.01)
    out[0] = omega * active
    out[1] = (par[12] - power - par[1] * omega) / (2.0 * par[0]) * active
    out[2] = (efd - eq_t - (par[5] - par[6]) * cur_d) / par[2] * active
    out[3] = (eq_t - eq_s - (par[6] - sub_x) * cur_d) / par[3] * active
    out[4] = ((par[8] - sub_x) * cur_q - ed_s) / par[4] * active
    out[5] = (par[9] * (par[11] - term) - efd) / par[10] * active

    all_back.wait_send()


def body(state, params, gen_count, gen_block, gen_local, impedance, fault_bus, cleared, fault_volt):
    dma = pltpu.SemaphoreType.DMA
    inputs = (
        state,
        params,
        gen_count,
        gen_block.reshape(1, SLOTS),
        gen_local.reshape(1, SLOTS),
        impedance.reshape(2, NZ // 2, BUS, 2 * BUS),
        fault_bus.reshape(1, SCN),
        cleared.reshape(1, SCN),
        fault_volt,
    )
    return pl.pallas_call(
        kernel,
        out_shape=jax.ShapeDtypeStruct(state.shape, F32),
        in_specs=[pl.BlockSpec(memory_space=pltpu.HBM)] * len(inputs),
        out_specs=pl.BlockSpec(memory_space=pltpu.VMEM),
        scratch_shapes=[
            (pltpu.SMEM if v.ndim == 1 else pltpu.VMEM)(v.shape, v.dtype) for v in inputs
        ]
        + [
            pltpu.VMEM((NZ // 2, 2 * BUS, 2 * BUS), BF16),
            pltpu.VMEM((NZ, NY, 3, 16, NNET * SCN), BF16),
            pltpu.VMEM((NGEN, 4, 128), F32),
            pltpu.VMEM((NGEN, 4, 128), F32),
            pltpu.VMEM((NNET, 16, 128), BF16),
            pltpu.VMEM((4, NNET, 16, 128), BF16),
            pltpu.VMEM((NX, NCORE, SCN, 2 * BUS), F32),
            pltpu.VMEM((NX, SCN, 2 * BUS), F32),
            pltpu.VMEM((NX, SCN, 2 * BUS), F32),
            pltpu.VMEM((NX, SCN, 2 * BUS), F32),
            pltpu.VMEM((NGEN, 4, 128), F32),
            pltpu.VMEM((NGEN, 4, 128), F32),
            pltpu.VMEM((4, SCN, SLOTS), F32),
            pltpu.VMEM((CAP * NGEN, BUS), BF16),
            pltpu.VMEM((SLOTS, CAP * NGEN), BF16),
            dma((9,)),
            dma,
            dma,
            dma((4,)),
            dma((4,)),
            dma((3, 4)),
            dma((3, 4)),
            dma,
            dma,
            dma,
            dma,
            dma,
            dma,
            dma,
            dma,
        ],
        compiler_params=pltpu.CompilerParams(
            collective_id=0, has_side_effects=True, vmem_limit_bytes=64 * 1024 * 1024 - 65536
        ),
    )(*inputs)


def solution(mesh):
    in_specs = (
        P(None, "net", "gen"),
        P(None, "gen"),
        P("gen"),
        P("gen", None),
        P("gen"),
        P(None, "net", "gen"),
        P("net"),
        P("net"),
        P(None, "net"),
    )
    return jax.shard_map(
        body, mesh=mesh, in_specs=in_specs, out_specs=P(None, "net", "gen"), check_vma=False
    )
```

```python
import functools

import jax
import jax.numpy as jnp
from jax import lax
from jax.experimental import pallas as pl
from jax.experimental.pallas import tpu as pltpu
from jax.sharding import PartitionSpec as P

F32 = jnp.float32
BF16 = jnp.bfloat16
NZ, NY, NX, NCORE = 16, 4, 4, 2
NGEN, NNET = NZ * NY, NX * NCORE
SCN = 32
SLOTS = 256
BUS = 192
SUB = BUS // NNET
CAP = 6
FAR = (0, 5, NZ - 5, NZ // 2)
BACK = (0, 2, 1, 3)
NEAR = (1, NZ - 1, 2, NZ - 2)
SIDE = (1, NY - 1, 2)
TILE = 128
NT = (((1,), (1,)), ((), ()))


def remote(src, dst, send_sem, recv_sem, gen, net):
    return pltpu.make_async_remote_copy(
        src_ref=src,
        dst_ref=dst,
        send_sem=send_sem,
        recv_sem=recv_sem,
        device_id=(gen, net),
        device_id_type=pl.DeviceIdType.MESH,
    )


def three(v):
    hi = v.astype(BF16)
    rest = v - hi.astype(F32)
    mid = rest.astype(BF16)
    lo = (rest - mid.astype(F32)).astype(BF16)
    return hi, mid, lo


def lane_iota(shape):
    return lax.broadcasted_iota(jnp.int32, shape, len(shape) - 1)


def row_iota(shape):
    return lax.broadcasted_iota(jnp.int32, shape, 0)


def pack(hot, vals):
    hi, mid, lo = three(vals)
    rhs = jnp.concatenate([hi, mid, lo, lo], axis=0)
    out = lax.dot_general(hot, rhs, NT, preferred_element_type=F32)
    left, right = out[:, :128], out[:, 128:]
    both = left + pltpu.roll(left, 64, 1) + right
    low = lane_iota((NGEN, 128)) < 64
    rows = []
    for j in range(CAP // 2):
        even = both[2 * j * NGEN : (2 * j + 1) * NGEN]
        odd = both[(2 * j + 1) * NGEN : (2 * j + 2) * NGEN]
        rows.append(jnp.where(low, even, odd))
    return rows


def unpack(hot, rows):
    every = jnp.concatenate(rows, axis=0)
    turned = pltpu.roll(every, 64, 1)
    low = lane_iota(every.shape) < 64
    vals = jnp.concatenate([jnp.where(low, every, turned), jnp.where(low, turned, every)], axis=0)
    hi, mid, lo = three(vals)
    first = jnp.where(lane_iota(vals.shape) < 64, hi.astype(F32), mid.astype(F32)).astype(BF16)
    rhs = jnp.concatenate([first, lo], axis=1)
    out = jnp.dot(hot, rhs, preferred_element_type=F32)
    left, right = out[:, :128], out[:, 128:]
    return left + pltpu.roll(left, 64, 1) + right


def kernel(
    state_h,
    params_h,
    count_h,
    block_h,
    local_h,
    z_hbm,
    fbus_h,
    cleared_h,
    fvolt_h,
    out,
    state,
    params,
    count,
    block,
    local,
    zbuf,
    fbus,
    cleared,
    fvolt,
    zt,
    gath,
    sbox,
    rbox,
    smsg,
    rmsg,
    vbuf,
    cbuf,
    wbuf,
    xbuf,
    sback,
    rback,
    keep,
    back_hot,
    slot_hot,
    in_sem,
    box_s,
    box_r,
    msg_s,
    msg_r,
    near_s,
    near_r,
    side_s,
    side_r,
    core_s,
    core_r,
    x_s,
    x_r,
    back_s,
    back_r,
):
    g = lax.axis_index("gen")
    n = lax.axis_index("net")
    z, y = g // NY, g % NY
    x, c = n // NCORE, n % NCORE
    barrier = pltpu.get_barrier_semaphore()

    def peer_at(i):
        zi, yi = i // NY, i % NY
        dz = NZ + NZ // 2 + ((zi + 1) // 2) * (2 * (zi % 2) - 1)
        dy = 2 + yi + yi // 2 + 2 * (yi // 3)
        return ((z + dz) % NZ) * NY + (y + dy) % NY

    def greet(gen, net):
        pl.semaphore_signal(
            barrier, inc=1, device_id=(gen, net), device_id_type=pl.DeviceIdType.MESH
        )

    def greet_gen(i, carry):
        greet(peer_at(i), n)
        return carry

    def greet_net(i, carry):
        greet(g, (n + i) % NNET)
        return carry

    lax.fori_loop(0, NGEN - 1, greet_gen, 0)
    lax.fori_loop(1, NNET, greet_net, 0)

    loads = [
        pltpu.make_async_copy(src, dst, in_sem.at[i])
        for i, (src, dst) in enumerate(
            [
                (block_h, block),
                (state_h, state),
                (params_h, params),
                (count_h, count),
                (local_h, local),
                (fbus_h, fbus),
                (cleared_h, cleared),
                (fvolt_h, fvolt),
                (z_hbm, zbuf),
            ]
        )
    ]
    for load in loads:
        load.start()

    loads[0].wait()
    tgt_l = block[...].astype(F32)
    ii, jj = row_iota((SLOTS, SLOTS)), lane_iota((SLOTS, SLOTS))
    same = jnp.broadcast_to(tgt_l, (SLOTS, SLOTS)).T == tgt_l
    rank_l = jnp.sum(jnp.where(same & (ii < jj), 1.0, 0.0), axis=0, keepdims=True)
    send_hot = jnp.where(
        row_iota((CAP * NGEN, SLOTS)).astype(F32) == rank_l * NGEN + tgt_l, 1.0, 0.0
    ).astype(BF16)
    for load in loads[1:8]:
        load.wait()

    active = (lane_iota((1, SLOTS)) < count[0]).astype(F32)
    delta, eq_s, ed_s = state[0], state[3], state[4]
    sin_d = jnp.sin(delta)
    cos_d = jnp.cos(delta)
    emf_re = ed_s * sin_d + eq_s * cos_d
    emf_im = eq_s * sin_d - ed_s * cos_d
    keep[0] = sin_d
    keep[1] = cos_d
    keep[2] = emf_re
    keep[3] = emf_im
    sub_x = params[7:8, :]
    cur = jnp.concatenate([emf_im / sub_x * active, -emf_re / sub_x * active], axis=0)
    for j, row in enumerate(pack(send_hot, cur)):
        sbox[:, j, :] = row
    ids = lax.dot_general(
        send_hot,
        jnp.broadcast_to((local[...] + 1).astype(F32), (128, SLOTS)).astype(BF16),
        NT,
        preferred_element_type=F32,
    )
    lane = lane_iota((NGEN, 128))
    id_row = jnp.zeros((NGEN, 128), F32)
    for r in range(CAP):
        id_row = jnp.where(lane == r, ids[r * NGEN : (r + 1) * NGEN], id_row)
    sbox[:, 3, :] = id_row

    pl.semaphore_wait(barrier, NGEN - 1 + NNET - 1)

    def send_box(i, carry):
        peer = peer_at(i)
        remote(sbox.at[peer], rbox.at[g], box_s, box_r, peer, n).start()
        return carry

    lax.fori_loop(0, NGEN - 1, send_box, 0)
    rbox[g] = sbox[g]
    loads[8].wait()

    def turn(j):
        parts = [zbuf[p, j].astype(F32) for p in range(2)]
        rows = []
        for k in range(8):
            a = k * SUB
            rows += [
                parts[0][a : a + 16],
                parts[1][a : a + 16],
                parts[0][a + 16 : a + 24],
                parts[1][a + 16 : a + 24],
            ]
        zt[j] = jnp.concatenate(rows, axis=0).T.astype(BF16)

    for j in range(5):
        turn(j)
    half = (rank_l.astype(jnp.int32) % 2) * (3 * NGEN) + (rank_l.astype(jnp.int32) // 2) * NGEN
    code = half.astype(F32) + tgt_l
    code_s = jnp.broadcast_to(code, (128, SLOTS)).T
    slot_hot[...] = jnp.concatenate(
        [
            jnp.where((lane_iota((SLOTS, 128)) + 128 * k).astype(F32) == code_s, 1.0, 0.0)
            for k in range(3)
        ],
        axis=1,
    ).astype(BF16)
    row = row_iota((256, 1))
    part, i16 = (row % 128) // 16, row % 16
    bus = part * SUB + jnp.where(row < 128, i16, 16 + i16 % 8)
    fb, cl = fbus[...], cleared[...]
    fb4 = jnp.concatenate([fb] * 4, axis=1)
    on4 = 1.0 - jnp.concatenate([cl] * 4, axis=1).astype(F32)
    fv4 = jnp.concatenate([fvolt[0:1], fvolt[1:2]] * 2, axis=1)
    fault = 10.0 * fv4 * (jnp.where(bus + g * BUS == fb4, 1.0, 0.0) * on4)

    all_boxes = remote(
        sbox.at[pl.ds(0, NGEN - 1)], rbox.at[pl.ds(0, NGEN - 1)], box_s, box_r, g, n
    )
    all_boxes.wait_recv()

    ids_in = rbox[:, 3, :]
    ids_t = ids_in.T
    id_lane = jnp.concatenate([ids_t[r : r + 1] for r in (0, 2, 4, 1, 3, 5)], axis=1)
    bus_hot = jnp.where((bus + 1).astype(F32) == id_lane, 1.0, 0.0).astype(BF16)
    summed = unpack(bus_hot, [rbox[:, j, :] for j in range(3)])
    inject = summed - fault
    first, second = inject[:128], inject[128:]
    i16 = row_iota((128, 128)) % 16
    second = jnp.where(i16 < 8, second, pltpu.roll(second, 96, 1))
    message = jnp.where(lane_iota((128, 128)) < 64, first, second).astype(BF16)
    smsg[...] = message.reshape(NNET, 16, 128)

    for k in (0, 1, 2, 3):

        def send_msg(i, carry, k=k):
            peer = (n + i) % NNET
            gen = ((z + FAR[k]) % NZ) * NY + y
            remote(smsg.at[peer], rmsg.at[BACK[k], n], msg_s.at[k], msg_r.at[BACK[k]], gen, peer).start()
            return carry

        lax.fori_loop(0 if k else 1, NNET, send_msg, 0)
    rmsg[0, n] = smsg[n]

    def all_msgs(k):
        count = NNET if k else NNET - 1
        return remote(
            smsg.at[pl.ds(0, count)], rmsg.at[k, pl.ds(0, count)], msg_s.at[k], msg_r.at[k], g, n
        )

    def near_copy(k, way):
        ref = gath.at[(z + FAR[k]) % NZ, y]
        return remote(
            ref, ref, near_s.at[way, k], near_r.at[way, k], ((z + NEAR[way]) % NZ) * NY + y, n
        )

    def send_sides(slot):
        for d in SIDE:
            ref = gath.at[slot, y]
            remote(ref, ref, side_s, side_r, z * NY + (y + d) % NY, n).start()

    def assemble(k):
        slot = (z + FAR[k]) % NZ
        all_msgs(k).wait_recv()
        tiles = [rmsg[k, m].astype(F32) for m in range(NNET)]
        for j in range(3):
            chunk = jnp.concatenate([t[:, SCN * j : SCN * (j + 1)] for t in tiles], axis=1)
            gath[slot, y, j] = chunk.astype(BF16)
        if k < 3:
            for way in (2, 3, 0, 1):
                near_copy(k, way).start()
        send_sides(slot)

    def arrive(k):
        for way in range(4):
            near_copy(k, way).wait_recv()
            send_sides((z + FAR[k] + NZ - NEAR[way]) % NZ)

    assemble(0)
    turn(5)
    assemble(1)
    assemble(2)
    turn(6)
    arrive(0)
    assemble(3)
    turn(7)
    bus_lane = lane_iota((NGEN, BUS)) + 1
    back_hot[...] = jnp.concatenate(
        [
            jnp.where(ids_in[:, r : r + 1].astype(jnp.int32) == bus_lane, 1.0, 0.0)
            for r in range(CAP)
        ],
        axis=0,
    ).astype(BF16)
    arrive(1)
    arrive(2)
    ref = gath.at[pl.ds(0, 3 * NZ // 4)]
    all_sides = remote(ref, ref, side_s, side_r, g, n)
    all_sides.wait_recv()

    sib = n + 1 - 2 * c
    tiles = range(2 * BUS // TILE)

    def core_copy(q):
        return remote(vbuf.at[q, :, 1 - c], cbuf.at[q], core_s.at[q], core_r.at[q], g, sib)

    def x_all(q):
        return remote(
            wbuf.at[q, pl.ds(0, NX - 1)],
            xbuf.at[q, pl.ds(0, NX - 1)],
            x_s.at[q],
            x_r.at[q],
            g,
            n,
        )

    def product(q):
        acc = jnp.zeros((TILE, NNET * SCN), F32)
        for j in range(NZ // 2):
            rows = gath[2 * j : 2 * j + 2].reshape(2 * BUS, NNET * SCN)
            acc = acc + jnp.dot(
                zt[j, TILE * q : TILE * (q + 1)], rows, preferred_element_type=F32
            )
        vbuf[q] = acc.T.reshape(NX, NCORE, SCN, TILE)
        core_copy(q).start()

    def add_core(q):
        core_copy(q).wait_recv()
        wbuf[q] = vbuf[q, :, c] + cbuf[q]
        for d in (2, 1, 3):
            peer = (x + d) % NX
            remote(
                wbuf.at[q, peer], xbuf.at[q, x], x_s.at[q], x_r.at[q], g, peer * NCORE + c
            ).start()
        xbuf[q, x] = wbuf[q, x]

    for q in tiles:
        product(q)
        if q:
            add_core(q - 1)
    add_core(tiles[-1])
    volts = []
    for q in tiles:
        x_all(q).wait_recv()
        volts.append((xbuf[q, 0] + xbuf[q, 1]) + (xbuf[q, 2] + xbuf[q, 3]))
    volts = jnp.concatenate(volts, axis=1)

    both = jnp.concatenate([volts[:, :BUS], volts[:, BUS:]], axis=0)
    for j, row in enumerate(pack(back_hot[...], both)):
        sback[:, j, :] = row

    def send_back(i, carry):
        peer = peer_at(i)
        remote(
            sback.at[peer, pl.ds(0, 3)], rback.at[g, pl.ds(0, 3)], back_s, back_r, peer, n
        ).start()
        return carry

    lax.fori_loop(0, NGEN - 1, send_back, 0)
    rback[g, 0:3] = sback[g, 0:3]

    all_boxes.wait_send()
    for k in range(4):
        all_msgs(k).wait_send()
        if k < 3:
            for way in range(4):
                near_copy(k, way).wait_send()
    all_sides.wait_send()
    for q in tiles:
        core_copy(q).wait_send()
        x_all(q).wait_send()

    all_back = remote(
        sback.at[pl.ds(0, NGEN - 1), pl.ds(0, 3)],
        rback.at[pl.ds(0, NGEN - 1), pl.ds(0, 3)],
        back_s,
        back_r,
        g,
        n,
    )
    all_back.wait_recv()
    at_gen = unpack(slot_hot[...], [rback[:, j, :] for j in range(3)]).T
    v_re, v_im = at_gen[:SCN], at_gen[SCN : 2 * SCN]

    sin_d, cos_d, emf_re, emf_im = keep[0], keep[1], keep[2], keep[3]
    omega, eq_t, eq_s, ed_s, efd = state[1], state[2], state[3], state[4], state[5]
    par = [params[k : k + 1, :] for k in range(13)]
    gen_re = (emf_im - v_im) / sub_x
    gen_im = (v_re - emf_re) / sub_x
    cur_d = gen_re * sin_d - gen_im * cos_d
    cur_q = gen_re * cos_d + gen_im * sin_d
    power = ed_s * cur_d + eq_s * cur_q
    term = jnp.sqrt(v_re * v_re + v_im * v_im + 0.01)
    out[0] = omega * active
    out[1] = (par[12] - power - par[1] * omega) / (2.0 * par[0]) * active
    out[2] = (efd - eq_t - (par[5] - par[6]) * cur_d) / par[2] * active
    out[3] = (eq_t - eq_s - (par[6] - sub_x) * cur_d) / par[3] * active
    out[4] = ((par[8] - sub_x) * cur_q - ed_s) / par[4] * active
    out[5] = (par[9] * (par[11] - term) - efd) / par[10] * active

    all_back.wait_send()


def body(state, params, gen_count, gen_block, gen_local, impedance, fault_bus, cleared, fault_volt):
    dma = pltpu.SemaphoreType.DMA
    inputs = (
        state,
        params,
        gen_count,
        gen_block.reshape(1, SLOTS),
        gen_local.reshape(1, SLOTS),
        impedance.reshape(2, NZ // 2, BUS, 2 * BUS),
        fault_bus.reshape(1, SCN),
        cleared.reshape(1, SCN),
        fault_volt,
    )
    return pl.pallas_call(
        kernel,
        out_shape=jax.ShapeDtypeStruct(state.shape, F32),
        in_specs=[pl.BlockSpec(memory_space=pltpu.HBM)] * len(inputs),
        out_specs=pl.BlockSpec(memory_space=pltpu.VMEM),
        scratch_shapes=[
            (pltpu.SMEM if v.ndim == 1 else pltpu.VMEM)(v.shape, v.dtype) for v in inputs
        ]
        + [
            pltpu.VMEM((NZ // 2, 2 * BUS, 2 * BUS), BF16),
            pltpu.VMEM((NZ, NY, 3, 16, NNET * SCN), BF16),
            pltpu.VMEM((NGEN, 4, 128), F32),
            pltpu.VMEM((NGEN, 4, 128), F32),
            pltpu.VMEM((NNET, 16, 128), BF16),
            pltpu.VMEM((4, NNET, 16, 128), BF16),
            pltpu.VMEM((2 * BUS // TILE, NX, NCORE, SCN, TILE), F32),
            pltpu.VMEM((2 * BUS // TILE, NX, SCN, TILE), F32),
            pltpu.VMEM((2 * BUS // TILE, NX, SCN, TILE), F32),
            pltpu.VMEM((2 * BUS // TILE, NX, SCN, TILE), F32),
            pltpu.VMEM((NGEN, 4, 128), F32),
            pltpu.VMEM((NGEN, 4, 128), F32),
            pltpu.VMEM((4, SCN, SLOTS), F32),
            pltpu.VMEM((CAP * NGEN, BUS), BF16),
            pltpu.VMEM((SLOTS, CAP * NGEN), BF16),
            dma((9,)),
            dma,
            dma,
            dma((4,)),
            dma((4,)),
            dma((4, 3)),
            dma((4, 3)),
            dma,
            dma,
            dma((2 * BUS // TILE,)),
            dma((2 * BUS // TILE,)),
            dma((2 * BUS // TILE,)),
            dma((2 * BUS // TILE,)),
            dma,
            dma,
        ],
        compiler_params=pltpu.CompilerParams(
            collective_id=0, has_side_effects=True, vmem_limit_bytes=64 * 1024 * 1024 - 65536
        ),
    )(*inputs)


def solution(mesh):
    in_specs = (
        P(None, "net", "gen"),
        P(None, "gen"),
        P("gen"),
        P("gen", None),
        P("gen"),
        P(None, "net", "gen"),
        P("net"),
        P("net"),
        P(None, "net"),
    )
    return jax.shard_map(
        body, mesh=mesh, in_specs=in_specs, out_specs=P(None, "net", "gen"), check_vma=False
    )
```

```python
import functools

import jax
import jax.numpy as jnp
from jax import lax
from jax.experimental import pallas as pl
from jax.experimental.pallas import tpu as pltpu
from jax.sharding import PartitionSpec as P

F32 = jnp.float32
BF16 = jnp.bfloat16
NZ, NY, NX, NCORE = 16, 4, 4, 2
NGEN, NNET = NZ * NY, NX * NCORE
SCN = 32
SLOTS = 256
BUS = 192
SUB = BUS // NNET
CAP = 6
FAR = (0, 5, NZ - 5, NZ // 2)
BACK = (0, 2, 1, 3)
NEAR = (1, NZ - 1, 2, NZ - 2)
SIDE = (1, NY - 1, 2)
RELAY = 8
TILE = 128
NT = (((1,), (1,)), ((), ()))


def remote(src, dst, send_sem, recv_sem, gen, net):
    return pltpu.make_async_remote_copy(
        src_ref=src,
        dst_ref=dst,
        send_sem=send_sem,
        recv_sem=recv_sem,
        device_id=(gen, net),
        device_id_type=pl.DeviceIdType.MESH,
    )


def three(v):
    hi = v.astype(BF16)
    rest = v - hi.astype(F32)
    mid = rest.astype(BF16)
    lo = (rest - mid.astype(F32)).astype(BF16)
    return hi, mid, lo


def lane_iota(shape):
    return lax.broadcasted_iota(jnp.int32, shape, len(shape) - 1)


def row_iota(shape):
    return lax.broadcasted_iota(jnp.int32, shape, 0)


def pack(hot, vals):
    hi, mid, lo = three(vals)
    rhs = jnp.concatenate([hi, mid, lo, lo], axis=0)
    out = lax.dot_general(hot, rhs, NT, preferred_element_type=F32)
    left, right = out[:, :128], out[:, 128:]
    both = left + pltpu.roll(left, 64, 1) + right
    low = lane_iota((NGEN, 128)) < 64
    rows = []
    for j in range(CAP // 2):
        even = both[2 * j * NGEN : (2 * j + 1) * NGEN]
        odd = both[(2 * j + 1) * NGEN : (2 * j + 2) * NGEN]
        rows.append(jnp.where(low, even, odd))
    return rows


def unpack(hot, rows):
    every = jnp.concatenate(rows, axis=0)
    turned = pltpu.roll(every, 64, 1)
    low = lane_iota(every.shape) < 64
    vals = jnp.concatenate([jnp.where(low, every, turned), jnp.where(low, turned, every)], axis=0)
    hi, mid, lo = three(vals)
    first = jnp.where(lane_iota(vals.shape) < 64, hi.astype(F32), mid.astype(F32)).astype(BF16)
    rhs = jnp.concatenate([first, lo], axis=1)
    out = jnp.dot(hot, rhs, preferred_element_type=F32)
    left, right = out[:, :128], out[:, 128:]
    return left + pltpu.roll(left, 64, 1) + right


def kernel(
    state_h,
    params_h,
    count_h,
    block_h,
    local_h,
    z_hbm,
    fbus_h,
    cleared_h,
    fvolt_h,
    out,
    state,
    params,
    count,
    block,
    local,
    zbuf,
    fbus,
    cleared,
    fvolt,
    zt,
    gath,
    sbox,
    rbox,
    smsg,
    rmsg,
    vbuf,
    cbuf,
    wbuf,
    xbuf,
    sback,
    rback,
    keep,
    back_hot,
    slot_hot,
    acc,
    in_sem,
    box_s,
    box_r,
    msg_s,
    msg_r,
    near_s,
    near_r,
    bundle_s,
    bundle_r,
    early_s,
    early_r,
    side_s,
    side_r,
    relay_s,
    relay_r,
    core_s,
    core_r,
    x_s,
    x_r,
    back_s,
    back_r,
):
    g = lax.axis_index("gen")
    n = lax.axis_index("net")
    z, y = g // NY, g % NY
    x, c = n // NCORE, n % NCORE
    barrier = pltpu.get_barrier_semaphore()

    def peer_at(i):
        zi, yi = i // NY, i % NY
        dz = NZ + NZ // 2 + ((zi + 1) // 2) * (2 * (zi % 2) - 1)
        dy = 2 + yi + yi // 2 + 2 * (yi // 3)
        return ((z + dz) % NZ) * NY + (y + dy) % NY

    def greet(gen, net):
        pl.semaphore_signal(
            barrier, inc=1, device_id=(gen, net), device_id_type=pl.DeviceIdType.MESH
        )

    def greet_gen(i, carry):
        greet(peer_at(i), n)
        return carry

    def greet_net(i, carry):
        greet(g, (n + i) % NNET)
        return carry

    lax.fori_loop(0, NGEN - 1, greet_gen, 0)
    lax.fori_loop(1, NNET, greet_net, 0)

    loads = [
        pltpu.make_async_copy(src, dst, in_sem.at[i])
        for i, (src, dst) in enumerate(
            [
                (block_h, block),
                (state_h, state),
                (params_h, params),
                (count_h, count),
                (local_h, local),
                (fbus_h, fbus),
                (cleared_h, cleared),
                (fvolt_h, fvolt),
                (z_hbm, zbuf),
            ]
        )
    ]
    for load in loads:
        load.start()

    loads[0].wait()
    tgt_l = block[...].astype(F32)
    ii, jj = row_iota((SLOTS, SLOTS)), lane_iota((SLOTS, SLOTS))
    same = jnp.broadcast_to(tgt_l, (SLOTS, SLOTS)).T == tgt_l
    rank_l = jnp.sum(jnp.where(same & (ii < jj), 1.0, 0.0), axis=0, keepdims=True)
    send_hot = jnp.where(
        row_iota((CAP * NGEN, SLOTS)).astype(F32) == rank_l * NGEN + tgt_l, 1.0, 0.0
    ).astype(BF16)
    for load in loads[1:8]:
        load.wait()

    active = (lane_iota((1, SLOTS)) < count[0]).astype(F32)
    delta, eq_s, ed_s = state[0], state[3], state[4]
    sin_d = jnp.sin(delta)
    cos_d = jnp.cos(delta)
    emf_re = ed_s * sin_d + eq_s * cos_d
    emf_im = eq_s * sin_d - ed_s * cos_d
    keep[0] = sin_d
    keep[1] = cos_d
    keep[2] = emf_re
    keep[3] = emf_im
    sub_x = params[7:8, :]
    cur = jnp.concatenate([emf_im / sub_x * active, -emf_re / sub_x * active], axis=0)
    for j, row in enumerate(pack(send_hot, cur)):
        sbox[:, j, :] = row
    ids = lax.dot_general(
        send_hot,
        jnp.broadcast_to((local[...] + 1).astype(F32), (128, SLOTS)).astype(BF16),
        NT,
        preferred_element_type=F32,
    )
    lane = lane_iota((NGEN, 128))
    id_row = jnp.zeros((NGEN, 128), F32)
    for r in range(CAP):
        id_row = jnp.where(lane == r, ids[r * NGEN : (r + 1) * NGEN], id_row)
    sbox[:, 3, :] = id_row

    pl.semaphore_wait(barrier, NGEN - 1 + NNET - 1)

    def send_box(i, carry):
        peer = peer_at(i)
        remote(sbox.at[peer], rbox.at[g], box_s, box_r, peer, n).start()
        return carry

    lax.fori_loop(0, NGEN - 1, send_box, 0)
    rbox[g] = sbox[g]
    loads[8].wait()

    def turn(j):
        parts = [zbuf[p, j].astype(F32) for p in range(2)]
        rows = []
        for k in range(8):
            a = k * SUB
            rows += [
                parts[0][a : a + 16],
                parts[1][a : a + 16],
                parts[0][a + 16 : a + 24],
                parts[1][a + 16 : a + 24],
            ]
        turned = jnp.concatenate(rows, axis=0).T.astype(BF16)
        zt[2 * j] = turned[:, :BUS]
        zt[2 * j + 1] = turned[:, BUS:]

    for j in range(5):
        turn(j)
    half = (rank_l.astype(jnp.int32) % 2) * (3 * NGEN) + (rank_l.astype(jnp.int32) // 2) * NGEN
    code = half.astype(F32) + tgt_l
    code_s = jnp.broadcast_to(code, (128, SLOTS)).T
    slot_hot[...] = jnp.concatenate(
        [
            jnp.where((lane_iota((SLOTS, 128)) + 128 * k).astype(F32) == code_s, 1.0, 0.0)
            for k in range(3)
        ],
        axis=1,
    ).astype(BF16)
    row = row_iota((256, 1))
    part, i16 = (row % 128) // 16, row % 16
    bus = part * SUB + jnp.where(row < 128, i16, 16 + i16 % 8)
    fb, cl = fbus[...], cleared[...]
    fb4 = jnp.concatenate([fb] * 4, axis=1)
    on4 = 1.0 - jnp.concatenate([cl] * 4, axis=1).astype(F32)
    fv4 = jnp.concatenate([fvolt[0:1], fvolt[1:2]] * 2, axis=1)
    fault = 10.0 * fv4 * (jnp.where(bus + g * BUS == fb4, 1.0, 0.0) * on4)

    all_boxes = remote(
        sbox.at[pl.ds(0, NGEN - 1)], rbox.at[pl.ds(0, NGEN - 1)], box_s, box_r, g, n
    )
    all_boxes.wait_recv()

    ids_in = rbox[:, 3, :]
    ids_t = ids_in.T
    id_lane = jnp.concatenate([ids_t[r : r + 1] for r in (0, 2, 4, 1, 3, 5)], axis=1)
    bus_hot = jnp.where((bus + 1).astype(F32) == id_lane, 1.0, 0.0).astype(BF16)
    summed = unpack(bus_hot, [rbox[:, j, :] for j in range(3)])
    inject = summed - fault
    first, second = inject[:128], inject[128:]
    i16 = row_iota((128, 128)) % 16
    second = jnp.where(i16 < 8, second, pltpu.roll(second, 96, 1))
    message = jnp.where(lane_iota((128, 128)) < 64, first, second).astype(BF16)
    smsg[...] = message.reshape(NNET, 16, 128)

    for k in (0, 1, 2, 3):

        def send_msg(i, carry, k=k):
            peer = (n + i) % NNET
            gen = ((z + FAR[k]) % NZ) * NY + y
            remote(smsg.at[peer], rmsg.at[BACK[k], n], msg_s.at[k], msg_r.at[BACK[k]], gen, peer).start()
            return carry

        lax.fori_loop(0 if k else 1, NNET, send_msg, 0)
    rmsg[0, n] = smsg[n]

    def all_msgs(k):
        count = NNET if k else NNET - 1
        return remote(
            smsg.at[pl.ds(0, count)], rmsg.at[k, pl.ds(0, count)], msg_s.at[k], msg_r.at[k], g, n
        )

    slots = [(z + FAR[k]) % NZ for k in range(3)]
    for k in (0, 3, 1, 2):
        if k == 3:
            slots.append((z + FAR[3]) % NZ)
        else:
            slots += [(z + FAR[k] + NZ - d) % NZ for d in NEAR]
    first = (0, 1, 2, 7)
    after = (3, 8, 12)

    def near_copy(k, way):
        ref = gath.at[slots[k], y, pl.ds(1, 2)]
        gen = ((z + NEAR[way]) % NZ) * NY + y
        return remote(ref, ref, near_s.at[way, k], near_r.at[way, k], gen, n)

    def bundle_copy(k, way):
        ref = gath.at[slots[k], :, 0]
        gen = ((z + NEAR[way]) % NZ) * NY + y
        return remote(ref, ref, bundle_s.at[way, k], bundle_r.at[way, k], gen, n)

    def early_copy(k, way):
        ref = gath.at[slots[first[k]], y, 0]
        gen = z * NY + (y + SIDE[way]) % NY
        return remote(ref, ref, early_s.at[way, k], early_r.at[way, k], gen, n)

    def side_copy(m, way):
        ref = gath.at[slots[m], y, pl.ds(1, 2)]
        gen = z * NY + (y + SIDE[way]) % NY
        return remote(ref, ref, side_s.at[way, m], side_r.at[way, m], gen, n)

    def relay_copy(m, way):
        ref = gath.at[slots[m], (y + SIDE[1 - way]) % NY, 1 + way]
        gen = z * NY + (y + SIDE[way]) % NY
        return remote(ref, ref, relay_s.at[way, m], relay_r.at[way, m], gen, n)

    def send_sides(m):
        for way in range(2 if m < RELAY else 3):
            side_copy(m, way).start()

    def relay(m):
        for way in range(2):
            side_copy(m, way).wait_recv()
            relay_copy(m, way).start()

    def assemble(k):
        all_msgs(k).wait_recv()
        tiles = [rmsg[k, m].astype(F32) for m in range(NNET)]
        for j in range(3):
            chunk = jnp.concatenate([t[:, SCN * j : SCN * (j + 1)] for t in tiles], axis=1)
            gath[slots[first[k]], y, j] = chunk.astype(BF16)
        for way in (2, 0, 1):
            early_copy(k, way).start()
        if k < 3:
            for way in (2, 3, 0, 1):
                near_copy(k, way).start()
        send_sides(first[k])

    def bundle(k):
        for way in range(3):
            early_copy(k, way).wait_recv()
        if k < 3:
            for way in (2, 3, 0, 1):
                bundle_copy(k, way).start()

    def arrive(k, way):
        near_copy(k, way).wait_recv()
        send_sides(after[k] + way)

    assemble(0)
    turn(5)
    for way in range(2):
        arrive(0, way)
    bundle(0)
    for way in range(2, 4):
        arrive(0, way)
    relay(0)
    assemble(1)
    assemble(2)
    assemble(3)
    turn(6)
    for m in (3, 4, 5, 6):
        relay(m)
    bundle(1)
    bundle(2)
    for way in range(4):
        arrive(1, way)
        if way < 3:
            relay((1, 2, 7)[way])
    for way in range(4):
        arrive(2, way)
    turn(7)
    bus_lane = lane_iota((NGEN, BUS)) + 1
    back_hot[...] = jnp.concatenate(
        [
            jnp.where(ids_in[:, r : r + 1].astype(jnp.int32) == bus_lane, 1.0, 0.0)
            for r in range(CAP)
        ],
        axis=0,
    ).astype(BF16)
    bundle(3)

    def product(group, rows=slice(None)):
        total = None
        for m in group:
            part = jnp.dot(
                zt[slots[m], rows],
                gath[slots[m]].reshape(BUS, NNET * SCN),
                preferred_element_type=F32,
            )
            total = part if total is None else total + part
        return total

    groups = (range(0, 4), range(4, 8), range(8, 12), range(12, 16))
    for i, group in enumerate(groups):
        for m in group:
            for way in range(2 if m < RELAY else 3):
                (relay_copy if m < RELAY else side_copy)(m, way).wait_recv()
            for k in range(3):
                if after[k] <= m < after[k] + 4:
                    bundle_copy(k, m - after[k]).wait_recv()
        if i == 0:
            acc[...] = product(group)
        elif i < 3:
            acc[...] += product(group)

    sib = n + 1 - 2 * c
    tiles = range(2 * BUS // TILE)

    def core_copy(q):
        return remote(vbuf.at[q, :, 1 - c], cbuf.at[q], core_s.at[q], core_r.at[q], g, sib)

    def x_all(q):
        return remote(
            wbuf.at[q, pl.ds(0, NX - 1)],
            xbuf.at[q, pl.ds(0, NX - 1)],
            x_s.at[q],
            x_r.at[q],
            g,
            n,
        )

    def finish(q):
        rows = slice(TILE * q, TILE * (q + 1))
        whole = acc[rows] + product(groups[3], rows)
        vbuf[q] = whole.T.reshape(NX, NCORE, SCN, TILE)
        core_copy(q).start()

    def add_core(q):
        core_copy(q).wait_recv()
        wbuf[q] = vbuf[q, :, c] + cbuf[q]
        for d in (2, 1, 3):
            peer = (x + d) % NX
            remote(
                wbuf.at[q, peer], xbuf.at[q, x], x_s.at[q], x_r.at[q], g, peer * NCORE + c
            ).start()
        xbuf[q, x] = wbuf[q, x]

    for q in tiles:
        finish(q)
        if q:
            add_core(q - 1)
    add_core(tiles[-1])
    volts = []
    for q in tiles:
        x_all(q).wait_recv()
        volts.append((xbuf[q, 0] + xbuf[q, 1]) + (xbuf[q, 2] + xbuf[q, 3]))
    volts = jnp.concatenate(volts, axis=1)

    both = jnp.concatenate([volts[:, :BUS], volts[:, BUS:]], axis=0)
    for j, row in enumerate(pack(back_hot[...], both)):
        sback[:, j, :] = row

    def send_back(i, carry):
        peer = peer_at(i)
        remote(
            sback.at[peer, pl.ds(0, 3)], rback.at[g, pl.ds(0, 3)], back_s, back_r, peer, n
        ).start()
        return carry

    lax.fori_loop(0, NGEN - 1, send_back, 0)
    rback[g, 0:3] = sback[g, 0:3]

    all_boxes.wait_send()
    for k in range(4):
        all_msgs(k).wait_send()
        for way in range(3):
            early_copy(k, way).wait_send()
        if k < 3:
            for way in range(4):
                near_copy(k, way).wait_send()
                bundle_copy(k, way).wait_send()
    for m in range(NZ):
        for way in range(2 if m < RELAY else 3):
            side_copy(m, way).wait_send()
            if m < RELAY:
                relay_copy(m, way).wait_send()
    for q in tiles:
        core_copy(q).wait_send()
        x_all(q).wait_send()

    all_back = remote(
        sback.at[pl.ds(0, NGEN - 1), pl.ds(0, 3)],
        rback.at[pl.ds(0, NGEN - 1), pl.ds(0, 3)],
        back_s,
        back_r,
        g,
        n,
    )
    all_back.wait_recv()
    at_gen = unpack(slot_hot[...], [rback[:, j, :] for j in range(3)]).T
    v_re, v_im = at_gen[:SCN], at_gen[SCN : 2 * SCN]

    sin_d, cos_d, emf_re, emf_im = keep[0], keep[1], keep[2], keep[3]
    omega, eq_t, eq_s, ed_s, efd = state[1], state[2], state[3], state[4], state[5]
    par = [params[k : k + 1, :] for k in range(13)]
    gen_re = (emf_im - v_im) / sub_x
    gen_im = (v_re - emf_re) / sub_x
    cur_d = gen_re * sin_d - gen_im * cos_d
    cur_q = gen_re * cos_d + gen_im * sin_d
    power = ed_s * cur_d + eq_s * cur_q
    term = jnp.sqrt(v_re * v_re + v_im * v_im + 0.01)
    out[0] = omega * active
    out[1] = (par[12] - power - par[1] * omega) / (2.0 * par[0]) * active
    out[2] = (efd - eq_t - (par[5] - par[6]) * cur_d) / par[2] * active
    out[3] = (eq_t - eq_s - (par[6] - sub_x) * cur_d) / par[3] * active
    out[4] = ((par[8] - sub_x) * cur_q - ed_s) / par[4] * active
    out[5] = (par[9] * (par[11] - term) - efd) / par[10] * active

    all_back.wait_send()


def body(state, params, gen_count, gen_block, gen_local, impedance, fault_bus, cleared, fault_volt):
    dma = pltpu.SemaphoreType.DMA
    inputs = (
        state,
        params,
        gen_count,
        gen_block.reshape(1, SLOTS),
        gen_local.reshape(1, SLOTS),
        impedance.reshape(2, NZ // 2, BUS, 2 * BUS),
        fault_bus.reshape(1, SCN),
        cleared.reshape(1, SCN),
        fault_volt,
    )
    return pl.pallas_call(
        kernel,
        out_shape=jax.ShapeDtypeStruct(state.shape, F32),
        in_specs=[pl.BlockSpec(memory_space=pltpu.HBM)] * len(inputs),
        out_specs=pl.BlockSpec(memory_space=pltpu.VMEM),
        scratch_shapes=[
            (pltpu.SMEM if v.ndim == 1 else pltpu.VMEM)(v.shape, v.dtype) for v in inputs
        ]
        + [
            pltpu.VMEM((NZ, 2 * BUS, BUS), BF16),
            pltpu.VMEM((NZ, NY, 3, 16, NNET * SCN), BF16),
            pltpu.VMEM((NGEN, 4, 128), F32),
            pltpu.VMEM((NGEN, 4, 128), F32),
            pltpu.VMEM((NNET, 16, 128), BF16),
            pltpu.VMEM((4, NNET, 16, 128), BF16),
            pltpu.VMEM((2 * BUS // TILE, NX, NCORE, SCN, TILE), F32),
            pltpu.VMEM((2 * BUS // TILE, NX, SCN, TILE), F32),
            pltpu.VMEM((2 * BUS // TILE, NX, SCN, TILE), F32),
            pltpu.VMEM((2 * BUS // TILE, NX, SCN, TILE), F32),
            pltpu.VMEM((NGEN, 4, 128), F32),
            pltpu.VMEM((NGEN, 4, 128), F32),
            pltpu.VMEM((4, SCN, SLOTS), F32),
            pltpu.VMEM((CAP * NGEN, BUS), BF16),
            pltpu.VMEM((SLOTS, CAP * NGEN), BF16),
            pltpu.VMEM((2 * BUS, NNET * SCN), F32),
            dma((9,)),
            dma,
            dma,
            dma((4,)),
            dma((4,)),
            dma((4, 3)),
            dma((4, 3)),
            dma((4, 3)),
            dma((4, 3)),
            dma((3, 4)),
            dma((3, 4)),
            dma((3, NZ)),
            dma((3, NZ)),
            dma((2, RELAY)),
            dma((2, RELAY)),
            dma((2 * BUS // TILE,)),
            dma((2 * BUS // TILE,)),
            dma((2 * BUS // TILE,)),
            dma((2 * BUS // TILE,)),
            dma,
            dma,
        ],
        compiler_params=pltpu.CompilerParams(
            collective_id=0, has_side_effects=True, vmem_limit_bytes=64 * 1024 * 1024 - 65536
        ),
    )(*inputs)


def solution(mesh):
    in_specs = (
        P(None, "net", "gen"),
        P(None, "gen"),
        P("gen"),
        P("gen", None),
        P("gen"),
        P(None, "net", "gen"),
        P("net"),
        P("net"),
        P(None, "net"),
    )
    return jax.shard_map(
        body, mesh=mesh, in_specs=in_specs, out_specs=P(None, "net", "gen"), check_vma=False
    )
```

```python
import functools

import jax
import jax.numpy as jnp
from jax import lax
from jax.experimental import pallas as pl
from jax.experimental.pallas import tpu as pltpu
from jax.sharding import PartitionSpec as P

F32 = jnp.float32
BF16 = jnp.bfloat16
NZ, NY, NX, NCORE = 16, 4, 4, 2
NGEN, NNET = NZ * NY, NX * NCORE
SCN = 32
SLOTS = 256
BUS = 192
SUB = BUS // NNET
CAP = 6
FAR = (0, 5, NZ - 5, NZ // 2)
BACK = (0, 2, 1, 3)
NEAR = (1, NZ - 1, 2, NZ - 2)
SIDE = (1, NY - 1, 2)
EARLY = (1, 2, 1, 1)
RELAY = (0, 3, 4, 5, 6, 7)
TILE = 128
NT = (((1,), (1,)), ((), ()))


def remote(src, dst, send_sem, recv_sem, gen, net):
    return pltpu.make_async_remote_copy(
        src_ref=src,
        dst_ref=dst,
        send_sem=send_sem,
        recv_sem=recv_sem,
        device_id=(gen, net),
        device_id_type=pl.DeviceIdType.MESH,
    )


def three(v):
    hi = v.astype(BF16)
    rest = v - hi.astype(F32)
    mid = rest.astype(BF16)
    lo = (rest - mid.astype(F32)).astype(BF16)
    return hi, mid, lo


def lane_iota(shape):
    return lax.broadcasted_iota(jnp.int32, shape, len(shape) - 1)


def row_iota(shape):
    return lax.broadcasted_iota(jnp.int32, shape, 0)


def pack(hot, vals):
    hi, mid, lo = three(vals)
    rhs = jnp.concatenate([hi, mid, lo, lo], axis=0)
    out = lax.dot_general(hot, rhs, NT, preferred_element_type=F32)
    left, right = out[:, :128], out[:, 128:]
    both = left + pltpu.roll(left, 64, 1) + right
    low = lane_iota((NGEN, 128)) < 64
    rows = []
    for j in range(CAP // 2):
        even = both[2 * j * NGEN : (2 * j + 1) * NGEN]
        odd = both[(2 * j + 1) * NGEN : (2 * j + 2) * NGEN]
        rows.append(jnp.where(low, even, odd))
    return rows


def unpack(hot, rows):
    every = jnp.concatenate(rows, axis=0)
    turned = pltpu.roll(every, 64, 1)
    low = lane_iota(every.shape) < 64
    vals = jnp.concatenate([jnp.where(low, every, turned), jnp.where(low, turned, every)], axis=0)
    hi, mid, lo = three(vals)
    first = jnp.where(lane_iota(vals.shape) < 64, hi.astype(F32), mid.astype(F32)).astype(BF16)
    rhs = jnp.concatenate([first, lo], axis=1)
    out = jnp.dot(hot, rhs, preferred_element_type=F32)
    left, right = out[:, :128], out[:, 128:]
    return left + pltpu.roll(left, 64, 1) + right


def kernel(
    state_h,
    params_h,
    count_h,
    block_h,
    local_h,
    z_hbm,
    fbus_h,
    cleared_h,
    fvolt_h,
    out,
    state,
    params,
    count,
    block,
    local,
    zbuf,
    fbus,
    cleared,
    fvolt,
    zt,
    gath,
    sbox,
    rbox,
    smsg,
    rmsg,
    vbuf,
    cbuf,
    wbuf,
    xbuf,
    sback,
    rback,
    keep,
    back_hot,
    slot_hot,
    acc,
    in_sem,
    box_s,
    box_r,
    msg_s,
    msg_r,
    near_s,
    near_r,
    bundle_s,
    bundle_r,
    early_s,
    early_r,
    side_s,
    side_r,
    relay_s,
    relay_r,
    core_s,
    core_r,
    x_s,
    x_r,
    back_s,
    back_r,
):
    g = lax.axis_index("gen")
    n = lax.axis_index("net")
    z, y = g // NY, g % NY
    x, c = n // NCORE, n % NCORE
    barrier = pltpu.get_barrier_semaphore()

    def peer_at(i):
        zi, yi = i // NY, i % NY
        dz = NZ + NZ // 2 + ((zi + 1) // 2) * (2 * (zi % 2) - 1)
        dy = 2 + yi + yi // 2 + 2 * (yi // 3)
        return ((z + dz) % NZ) * NY + (y + dy) % NY

    def greet(gen, net):
        pl.semaphore_signal(
            barrier, inc=1, device_id=(gen, net), device_id_type=pl.DeviceIdType.MESH
        )

    def greet_gen(i, carry):
        greet(peer_at(i), n)
        return carry

    def greet_net(i, carry):
        greet(g, (n + i) % NNET)
        return carry

    lax.fori_loop(0, NGEN - 1, greet_gen, 0)
    lax.fori_loop(1, NNET, greet_net, 0)

    loads = [
        pltpu.make_async_copy(src, dst, in_sem.at[i])
        for i, (src, dst) in enumerate(
            [
                (block_h, block),
                (state_h, state),
                (params_h, params),
                (count_h, count),
                (local_h, local),
                (fbus_h, fbus),
                (cleared_h, cleared),
                (fvolt_h, fvolt),
                (z_hbm, zbuf),
            ]
        )
    ]
    for load in loads:
        load.start()

    loads[0].wait()
    tgt_l = block[...].astype(F32)
    ii, jj = row_iota((SLOTS, SLOTS)), lane_iota((SLOTS, SLOTS))
    same = jnp.broadcast_to(tgt_l, (SLOTS, SLOTS)).T == tgt_l
    rank_l = jnp.sum(jnp.where(same & (ii < jj), 1.0, 0.0), axis=0, keepdims=True)
    send_hot = jnp.where(
        row_iota((CAP * NGEN, SLOTS)).astype(F32) == rank_l * NGEN + tgt_l, 1.0, 0.0
    ).astype(BF16)
    for load in loads[1:8]:
        load.wait()

    active = (lane_iota((1, SLOTS)) < count[0]).astype(F32)
    delta, eq_s, ed_s = state[0], state[3], state[4]
    sin_d = jnp.sin(delta)
    cos_d = jnp.cos(delta)
    emf_re = ed_s * sin_d + eq_s * cos_d
    emf_im = eq_s * sin_d - ed_s * cos_d
    keep[0] = sin_d
    keep[1] = cos_d
    keep[2] = emf_re
    keep[3] = emf_im
    sub_x = params[7:8, :]
    cur = jnp.concatenate([emf_im / sub_x * active, -emf_re / sub_x * active], axis=0)
    for j, row in enumerate(pack(send_hot, cur)):
        sbox[:, j, :] = row
    ids = lax.dot_general(
        send_hot,
        jnp.broadcast_to((local[...] + 1).astype(F32), (128, SLOTS)).astype(BF16),
        NT,
        preferred_element_type=F32,
    )
    lane = lane_iota((NGEN, 128))
    id_row = jnp.zeros((NGEN, 128), F32)
    for r in range(CAP):
        id_row = jnp.where(lane == r, ids[r * NGEN : (r + 1) * NGEN], id_row)
    sbox[:, 3, :] = id_row

    pl.semaphore_wait(barrier, NGEN - 1 + NNET - 1)

    def send_box(i, carry):
        peer = peer_at(i)
        remote(sbox.at[peer], rbox.at[g], box_s, box_r, peer, n).start()
        return carry

    lax.fori_loop(0, NGEN - 1, send_box, 0)
    rbox[g] = sbox[g]
    loads[8].wait()

    def turn(j):
        parts = [zbuf[p, j].astype(F32) for p in range(2)]
        rows = []
        for k in range(8):
            a = k * SUB
            rows += [
                parts[0][a : a + 16],
                parts[1][a : a + 16],
                parts[0][a + 16 : a + 24],
                parts[1][a + 16 : a + 24],
            ]
        turned = jnp.concatenate(rows, axis=0).T.astype(BF16)
        zt[2 * j] = turned[:, :BUS]
        zt[2 * j + 1] = turned[:, BUS:]

    for j in range(5):
        turn(j)
    half = (rank_l.astype(jnp.int32) % 2) * (3 * NGEN) + (rank_l.astype(jnp.int32) // 2) * NGEN
    code = half.astype(F32) + tgt_l
    code_s = jnp.broadcast_to(code, (128, SLOTS)).T
    slot_hot[...] = jnp.concatenate(
        [
            jnp.where((lane_iota((SLOTS, 128)) + 128 * k).astype(F32) == code_s, 1.0, 0.0)
            for k in range(3)
        ],
        axis=1,
    ).astype(BF16)
    row = row_iota((256, 1))
    part, i16 = (row % 128) // 16, row % 16
    bus = part * SUB + jnp.where(row < 128, i16, 16 + i16 % 8)
    fb, cl = fbus[...], cleared[...]
    fb4 = jnp.concatenate([fb] * 4, axis=1)
    on4 = 1.0 - jnp.concatenate([cl] * 4, axis=1).astype(F32)
    fv4 = jnp.concatenate([fvolt[0:1], fvolt[1:2]] * 2, axis=1)
    fault = 10.0 * fv4 * (jnp.where(bus + g * BUS == fb4, 1.0, 0.0) * on4)

    all_boxes = remote(
        sbox.at[pl.ds(0, NGEN - 1)], rbox.at[pl.ds(0, NGEN - 1)], box_s, box_r, g, n
    )
    all_boxes.wait_recv()

    ids_in = rbox[:, 3, :]
    ids_t = ids_in.T
    id_lane = jnp.concatenate([ids_t[r : r + 1] for r in (0, 2, 4, 1, 3, 5)], axis=1)
    bus_hot = jnp.where((bus + 1).astype(F32) == id_lane, 1.0, 0.0).astype(BF16)
    summed = unpack(bus_hot, [rbox[:, j, :] for j in range(3)])
    inject = summed - fault
    first, second = inject[:128], inject[128:]
    i16 = row_iota((128, 128)) % 16
    second = jnp.where(i16 < 8, second, pltpu.roll(second, 96, 1))
    message = jnp.where(lane_iota((128, 128)) < 64, first, second).astype(BF16)
    smsg[...] = message.reshape(NNET, 16, 128)

    for k in (0, 1, 2, 3):

        def send_msg(i, carry, k=k):
            peer = (n + i) % NNET
            gen = ((z + FAR[k]) % NZ) * NY + y
            remote(smsg.at[peer], rmsg.at[BACK[k], n], msg_s.at[k], msg_r.at[BACK[k]], gen, peer).start()
            return carry

        lax.fori_loop(0 if k else 1, NNET, send_msg, 0)
    rmsg[0, n] = smsg[n]

    def all_msgs(k):
        count = NNET if k else NNET - 1
        return remote(
            smsg.at[pl.ds(0, count)], rmsg.at[k, pl.ds(0, count)], msg_s.at[k], msg_r.at[k], g, n
        )

    slots = [(z + FAR[k]) % NZ for k in range(3)]
    for k in (0, 3, 1, 2):
        if k == 3:
            slots.append((z + FAR[3]) % NZ)
        else:
            slots += [(z + FAR[k] + NZ - d) % NZ for d in NEAR]
    origin = (0, 1, 2, 7)
    source = (0, 1, 2, 0, 0, 0, 0, 3, 1, 1, 1, 1, 2, 2, 2, 2)
    after = (3, 8, 12)

    def late(k):
        return pl.ds(EARLY[k], 3 - EARLY[k])

    def near_copy(k, way):
        ref = gath.at[slots[k], y, late(k)]
        gen = ((z + NEAR[way]) % NZ) * NY + y
        return remote(ref, ref, near_s.at[way, k], near_r.at[way, k], gen, n)

    def bundle_copy(k, way):
        ref = gath.at[slots[k], :, pl.ds(0, EARLY[k])]
        gen = ((z + NEAR[way]) % NZ) * NY + y
        return remote(ref, ref, bundle_s.at[way, k], bundle_r.at[way, k], gen, n)

    def early_copy(k, way):
        ref = gath.at[slots[origin[k]], y, pl.ds(0, EARLY[k])]
        gen = z * NY + (y + SIDE[way]) % NY
        return remote(ref, ref, early_s.at[way, k], early_r.at[way, k], gen, n)

    def side_copy(m, way):
        ref = gath.at[slots[m], y, late(source[m])]
        gen = z * NY + (y + SIDE[way]) % NY
        return remote(ref, ref, side_s.at[way, m], side_r.at[way, m], gen, n)

    def relay_copy(m, way):
        ref = gath.at[slots[m], (y + SIDE[1 - way]) % NY, 1 + way]
        gen = z * NY + (y + SIDE[way]) % NY
        return remote(ref, ref, relay_s.at[way, m], relay_r.at[way, m], gen, n)

    def send_sides(m):
        for way in range(2 if m in RELAY else 3):
            side_copy(m, way).start()

    def relay(m):
        for way in range(2):
            side_copy(m, way).wait_recv()
            relay_copy(m, way).start()

    def assemble(k):
        all_msgs(k).wait_recv()
        tiles = [rmsg[k, m].astype(F32) for m in range(NNET)]
        for j in range(3):
            chunk = jnp.concatenate([t[:, SCN * j : SCN * (j + 1)] for t in tiles], axis=1)
            gath[slots[origin[k]], y, j] = chunk.astype(BF16)
        for way in (2, 0, 1):
            early_copy(k, way).start()
        if k < 3:
            for way in (2, 3, 0, 1):
                near_copy(k, way).start()
        send_sides(origin[k])

    def bundle(k):
        for way in range(3):
            early_copy(k, way).wait_recv()
        if k < 3:
            for way in (2, 3, 0, 1):
                bundle_copy(k, way).start()

    def arrive(k, way):
        near_copy(k, way).wait_recv()
        send_sides(after[k] + way)

    assemble(0)
    turn(5)
    for way in range(2):
        arrive(0, way)
    bundle(0)
    for way in range(2, 4):
        arrive(0, way)
    relay(0)
    assemble(1)
    assemble(2)
    assemble(3)
    turn(6)
    for m in (3, 4, 5, 6):
        relay(m)
    bundle(1)
    bundle(2)
    for way in range(4):
        arrive(1, way)
    relay(7)
    for way in range(4):
        arrive(2, way)
    turn(7)
    bus_lane = lane_iota((NGEN, BUS)) + 1
    back_hot[...] = jnp.concatenate(
        [
            jnp.where(ids_in[:, r : r + 1].astype(jnp.int32) == bus_lane, 1.0, 0.0)
            for r in range(CAP)
        ],
        axis=0,
    ).astype(BF16)
    bundle(3)

    def product(group, rows=slice(None)):
        total = None
        for m in group:
            part = jnp.dot(
                zt[slots[m], rows],
                gath[slots[m]].reshape(BUS, NNET * SCN),
                preferred_element_type=F32,
            )
            total = part if total is None else total + part
        return total

    groups = (range(0, 4), range(4, 8), range(8, 12), range(12, 16))
    for i, group in enumerate(groups):
        for m in group:
            for way in range(2 if m in RELAY else 3):
                (relay_copy if m in RELAY else side_copy)(m, way).wait_recv()
            for k in range(3):
                if after[k] <= m < after[k] + 4:
                    bundle_copy(k, m - after[k]).wait_recv()
        if i == 0:
            acc[...] = product(group)
        elif i < 3:
            acc[...] += product(group)

    sib = n + 1 - 2 * c
    tiles = range(2 * BUS // TILE)

    def core_copy(q):
        return remote(vbuf.at[q, :, 1 - c], cbuf.at[q], core_s.at[q], core_r.at[q], g, sib)

    def x_all(q):
        return remote(
            wbuf.at[q, pl.ds(0, NX - 1)],
            xbuf.at[q, pl.ds(0, NX - 1)],
            x_s.at[q],
            x_r.at[q],
            g,
            n,
        )

    def finish(q):
        rows = slice(TILE * q, TILE * (q + 1))
        whole = acc[rows] + product(groups[3], rows)
        vbuf[q] = whole.T.reshape(NX, NCORE, SCN, TILE)
        core_copy(q).start()

    def add_core(q):
        core_copy(q).wait_recv()
        wbuf[q] = vbuf[q, :, c] + cbuf[q]
        for d in (2, 1, 3):
            peer = (x + d) % NX
            remote(
                wbuf.at[q, peer], xbuf.at[q, x], x_s.at[q], x_r.at[q], g, peer * NCORE + c
            ).start()
        xbuf[q, x] = wbuf[q, x]

    for q in tiles:
        finish(q)
        if q:
            add_core(q - 1)
    add_core(tiles[-1])
    volts = []
    for q in tiles:
        x_all(q).wait_recv()
        volts.append((xbuf[q, 0] + xbuf[q, 1]) + (xbuf[q, 2] + xbuf[q, 3]))
    volts = jnp.concatenate(volts, axis=1)

    both = jnp.concatenate([volts[:, :BUS], volts[:, BUS:]], axis=0)
    for j, row in enumerate(pack(back_hot[...], both)):
        sback[:, j, :] = row

    def send_back(i, carry):
        peer = peer_at(i)
        remote(
            sback.at[peer, pl.ds(0, 3)], rback.at[g, pl.ds(0, 3)], back_s, back_r, peer, n
        ).start()
        return carry

    lax.fori_loop(0, NGEN - 1, send_back, 0)
    rback[g, 0:3] = sback[g, 0:3]

    all_boxes.wait_send()
    for k in range(4):
        all_msgs(k).wait_send()
        for way in range(3):
            early_copy(k, way).wait_send()
        if k < 3:
            for way in range(4):
                near_copy(k, way).wait_send()
                bundle_copy(k, way).wait_send()
    for m in range(NZ):
        for way in range(2 if m in RELAY else 3):
            side_copy(m, way).wait_send()
            if m in RELAY:
                relay_copy(m, way).wait_send()
    for q in tiles:
        core_copy(q).wait_send()
        x_all(q).wait_send()

    all_back = remote(
        sback.at[pl.ds(0, NGEN - 1), pl.ds(0, 3)],
        rback.at[pl.ds(0, NGEN - 1), pl.ds(0, 3)],
        back_s,
        back_r,
        g,
        n,
    )
    all_back.wait_recv()
    at_gen = unpack(slot_hot[...], [rback[:, j, :] for j in range(3)]).T
    v_re, v_im = at_gen[:SCN], at_gen[SCN : 2 * SCN]

    sin_d, cos_d, emf_re, emf_im = keep[0], keep[1], keep[2], keep[3]
    omega, eq_t, eq_s, ed_s, efd = state[1], state[2], state[3], state[4], state[5]
    par = [params[k : k + 1, :] for k in range(13)]
    gen_re = (emf_im - v_im) / sub_x
    gen_im = (v_re - emf_re) / sub_x
    cur_d = gen_re * sin_d - gen_im * cos_d
    cur_q = gen_re * cos_d + gen_im * sin_d
    power = ed_s * cur_d + eq_s * cur_q
    term = jnp.sqrt(v_re * v_re + v_im * v_im + 0.01)
    out[0] = omega * active
    out[1] = (par[12] - power - par[1] * omega) / (2.0 * par[0]) * active
    out[2] = (efd - eq_t - (par[5] - par[6]) * cur_d) / par[2] * active
    out[3] = (eq_t - eq_s - (par[6] - sub_x) * cur_d) / par[3] * active
    out[4] = ((par[8] - sub_x) * cur_q - ed_s) / par[4] * active
    out[5] = (par[9] * (par[11] - term) - efd) / par[10] * active

    all_back.wait_send()


def body(state, params, gen_count, gen_block, gen_local, impedance, fault_bus, cleared, fault_volt):
    dma = pltpu.SemaphoreType.DMA
    inputs = (
        state,
        params,
        gen_count,
        gen_block.reshape(1, SLOTS),
        gen_local.reshape(1, SLOTS),
        impedance.reshape(2, NZ // 2, BUS, 2 * BUS),
        fault_bus.reshape(1, SCN),
        cleared.reshape(1, SCN),
        fault_volt,
    )
    return pl.pallas_call(
        kernel,
        out_shape=jax.ShapeDtypeStruct(state.shape, F32),
        in_specs=[pl.BlockSpec(memory_space=pltpu.HBM)] * len(inputs),
        out_specs=pl.BlockSpec(memory_space=pltpu.VMEM),
        scratch_shapes=[
            (pltpu.SMEM if v.ndim == 1 else pltpu.VMEM)(v.shape, v.dtype) for v in inputs
        ]
        + [
            pltpu.VMEM((NZ, 2 * BUS, BUS), BF16),
            pltpu.VMEM((NZ, NY, 3, 16, NNET * SCN), BF16),
            pltpu.VMEM((NGEN, 4, 128), F32),
            pltpu.VMEM((NGEN, 4, 128), F32),
            pltpu.VMEM((NNET, 16, 128), BF16),
            pltpu.VMEM((4, NNET, 16, 128), BF16),
            pltpu.VMEM((2 * BUS // TILE, NX, NCORE, SCN, TILE), F32),
            pltpu.VMEM((2 * BUS // TILE, NX, SCN, TILE), F32),
            pltpu.VMEM((2 * BUS // TILE, NX, SCN, TILE), F32),
            pltpu.VMEM((2 * BUS // TILE, NX, SCN, TILE), F32),
            pltpu.VMEM((NGEN, 4, 128), F32),
            pltpu.VMEM((NGEN, 4, 128), F32),
            pltpu.VMEM((4, SCN, SLOTS), F32),
            pltpu.VMEM((CAP * NGEN, BUS), BF16),
            pltpu.VMEM((SLOTS, CAP * NGEN), BF16),
            pltpu.VMEM((2 * BUS, NNET * SCN), F32),
            dma((9,)),
            dma,
            dma,
            dma((4,)),
            dma((4,)),
            dma((4, 3)),
            dma((4, 3)),
            dma((4, 3)),
            dma((4, 3)),
            dma((3, 4)),
            dma((3, 4)),
            dma((3, NZ)),
            dma((3, NZ)),
            dma((2, NZ)),
            dma((2, NZ)),
            dma((2 * BUS // TILE,)),
            dma((2 * BUS // TILE,)),
            dma((2 * BUS // TILE,)),
            dma((2 * BUS // TILE,)),
            dma,
            dma,
        ],
        compiler_params=pltpu.CompilerParams(
            collective_id=0, has_side_effects=True, vmem_limit_bytes=64 * 1024 * 1024 - 65536
        ),
    )(*inputs)


def solution(mesh):
    in_specs = (
        P(None, "net", "gen"),
        P(None, "gen"),
        P("gen"),
        P("gen", None),
        P("gen"),
        P(None, "net", "gen"),
        P("net"),
        P("net"),
        P(None, "net"),
    )
    return jax.shard_map(
        body, mesh=mesh, in_specs=in_specs, out_specs=P(None, "net", "gen"), check_vma=False
    )
```

```python
import functools

import jax
import jax.numpy as jnp
from jax import lax
from jax.experimental import pallas as pl
from jax.experimental.pallas import tpu as pltpu
from jax.sharding import PartitionSpec as P

F32 = jnp.float32
BF16 = jnp.bfloat16
NZ, NY, NX, NCORE = 16, 4, 4, 2
NGEN, NNET = NZ * NY, NX * NCORE
SCN = 32
SLOTS = 256
BUS = 192
SUB = BUS // NNET
CAP = 6
FAR = (0, 5, NZ - 5, NZ // 2)
BACK = (0, 2, 1)
NEAR = (1, NZ - 1, 2, NZ - 2)
SIDE = (1, NY - 1, 2)
EARLY = (1, 2, 1, 1)
RELAY = (0, 3, 4, 5, 6, 7)
TILE = 128
NT = (((1,), (1,)), ((), ()))


def remote(src, dst, send_sem, recv_sem, gen, net):
    return pltpu.make_async_remote_copy(
        src_ref=src,
        dst_ref=dst,
        send_sem=send_sem,
        recv_sem=recv_sem,
        device_id=(gen, net),
        device_id_type=pl.DeviceIdType.MESH,
    )


def three(v):
    hi = v.astype(BF16)
    rest = v - hi.astype(F32)
    mid = rest.astype(BF16)
    lo = (rest - mid.astype(F32)).astype(BF16)
    return hi, mid, lo


def lane_iota(shape):
    return lax.broadcasted_iota(jnp.int32, shape, len(shape) - 1)


def row_iota(shape):
    return lax.broadcasted_iota(jnp.int32, shape, 0)


def pack(hot, vals):
    hi, mid, lo = three(vals)
    rhs = jnp.concatenate([hi, mid, lo, lo], axis=0)
    out = lax.dot_general(hot, rhs, NT, preferred_element_type=F32)
    left, right = out[:, :128], out[:, 128:]
    both = left + pltpu.roll(left, 64, 1) + right
    low = lane_iota((NGEN, 128)) < 64
    rows = []
    for j in range(CAP // 2):
        even = both[2 * j * NGEN : (2 * j + 1) * NGEN]
        odd = both[(2 * j + 1) * NGEN : (2 * j + 2) * NGEN]
        rows.append(jnp.where(low, even, odd))
    return rows


def unpack(hot, rows):
    every = jnp.concatenate(rows, axis=0)
    turned = pltpu.roll(every, 64, 1)
    low = lane_iota(every.shape) < 64
    vals = jnp.concatenate([jnp.where(low, every, turned), jnp.where(low, turned, every)], axis=0)
    hi, mid, lo = three(vals)
    first = jnp.where(lane_iota(vals.shape) < 64, hi.astype(F32), mid.astype(F32)).astype(BF16)
    rhs = jnp.concatenate([first, lo], axis=1)
    out = jnp.dot(hot, rhs, preferred_element_type=F32)
    left, right = out[:, :128], out[:, 128:]
    return left + pltpu.roll(left, 64, 1) + right


def kernel(
    state_h,
    params_h,
    count_h,
    block_h,
    local_h,
    z_hbm,
    fbus_h,
    cleared_h,
    fvolt_h,
    out,
    state,
    params,
    count,
    block,
    local,
    zbuf,
    fbus,
    cleared,
    fvolt,
    zt,
    gath,
    sbox,
    rbox,
    smsg,
    rmsg,
    vbuf,
    cbuf,
    wbuf,
    xbuf,
    sback,
    rback,
    keep,
    back_hot,
    slot_hot,
    acc,
    in_sem,
    box_s,
    box_r,
    msg_s,
    msg_r,
    far_s,
    far_r,
    near_s,
    near_r,
    bundle_s,
    bundle_r,
    early_s,
    early_r,
    side_s,
    side_r,
    relay_s,
    relay_r,
    core_s,
    core_r,
    x_s,
    x_r,
    back_s,
    back_r,
):
    g = lax.axis_index("gen")
    n = lax.axis_index("net")
    z, y = g // NY, g % NY
    x, c = n // NCORE, n % NCORE
    barrier = pltpu.get_barrier_semaphore()

    def peer_at(i):
        zi, yi = i // NY, i % NY
        dz = NZ + NZ // 2 + ((zi + 1) // 2) * (2 * (zi % 2) - 1)
        dy = 2 + yi + yi // 2 + 2 * (yi // 3)
        return ((z + dz) % NZ) * NY + (y + dy) % NY

    def greet(gen, net):
        pl.semaphore_signal(
            barrier, inc=1, device_id=(gen, net), device_id_type=pl.DeviceIdType.MESH
        )

    def greet_gen(i, carry):
        greet(peer_at(i), n)
        return carry

    def greet_net(i, carry):
        greet(g, (n + i) % NNET)
        return carry

    lax.fori_loop(0, NGEN - 1, greet_gen, 0)
    lax.fori_loop(1, NNET, greet_net, 0)

    loads = [
        pltpu.make_async_copy(src, dst, in_sem.at[i])
        for i, (src, dst) in enumerate(
            [
                (block_h, block),
                (state_h, state),
                (params_h, params),
                (count_h, count),
                (local_h, local),
                (fbus_h, fbus),
                (cleared_h, cleared),
                (fvolt_h, fvolt),
                (z_hbm, zbuf),
            ]
        )
    ]
    for load in loads:
        load.start()

    loads[0].wait()
    tgt_l = block[...].astype(F32)
    ii, jj = row_iota((SLOTS, SLOTS)), lane_iota((SLOTS, SLOTS))
    same = jnp.broadcast_to(tgt_l, (SLOTS, SLOTS)).T == tgt_l
    rank_l = jnp.sum(jnp.where(same & (ii < jj), 1.0, 0.0), axis=0, keepdims=True)
    send_hot = jnp.where(
        row_iota((CAP * NGEN, SLOTS)).astype(F32) == rank_l * NGEN + tgt_l, 1.0, 0.0
    ).astype(BF16)
    for load in loads[1:8]:
        load.wait()

    active = (lane_iota((1, SLOTS)) < count[0]).astype(F32)
    delta, eq_s, ed_s = state[0], state[3], state[4]
    sin_d = jnp.sin(delta)
    cos_d = jnp.cos(delta)
    emf_re = ed_s * sin_d + eq_s * cos_d
    emf_im = eq_s * sin_d - ed_s * cos_d
    keep[0] = sin_d
    keep[1] = cos_d
    keep[2] = emf_re
    keep[3] = emf_im
    sub_x = params[7:8, :]
    cur = jnp.concatenate([emf_im / sub_x * active, -emf_re / sub_x * active], axis=0)
    for j, row in enumerate(pack(send_hot, cur)):
        sbox[:, j, :] = row
    ids = lax.dot_general(
        send_hot,
        jnp.broadcast_to((local[...] + 1).astype(F32), (128, SLOTS)).astype(BF16),
        NT,
        preferred_element_type=F32,
    )
    lane = lane_iota((NGEN, 128))
    id_row = jnp.zeros((NGEN, 128), F32)
    for r in range(CAP):
        id_row = jnp.where(lane == r, ids[r * NGEN : (r + 1) * NGEN], id_row)
    sbox[:, 3, :] = id_row

    pl.semaphore_wait(barrier, NGEN - 1 + NNET - 1)

    def send_box(i, carry):
        peer = peer_at(i)
        remote(sbox.at[peer], rbox.at[g], box_s, box_r, peer, n).start()
        return carry

    lax.fori_loop(0, NGEN - 1, send_box, 0)
    rbox[g] = sbox[g]
    loads[8].wait()

    def turn(j):
        parts = [zbuf[p, j].astype(F32) for p in range(2)]
        rows = []
        for k in range(8):
            a = k * SUB
            rows += [
                parts[0][a : a + 16],
                parts[1][a : a + 16],
                parts[0][a + 16 : a + 24],
                parts[1][a + 16 : a + 24],
            ]
        turned = jnp.concatenate(rows, axis=0).T.astype(BF16)
        zt[2 * j] = turned[:, :BUS]
        zt[2 * j + 1] = turned[:, BUS:]

    for j in range(5):
        turn(j)
    half = (rank_l.astype(jnp.int32) % 2) * (3 * NGEN) + (rank_l.astype(jnp.int32) // 2) * NGEN
    code = half.astype(F32) + tgt_l
    code_s = jnp.broadcast_to(code, (128, SLOTS)).T
    slot_hot[...] = jnp.concatenate(
        [
            jnp.where((lane_iota((SLOTS, 128)) + 128 * k).astype(F32) == code_s, 1.0, 0.0)
            for k in range(3)
        ],
        axis=1,
    ).astype(BF16)
    row = row_iota((256, 1))
    part, i16 = (row % 128) // 16, row % 16
    bus = part * SUB + jnp.where(row < 128, i16, 16 + i16 % 8)
    fb, cl = fbus[...], cleared[...]
    fb4 = jnp.concatenate([fb] * 4, axis=1)
    on4 = 1.0 - jnp.concatenate([cl] * 4, axis=1).astype(F32)
    fv4 = jnp.concatenate([fvolt[0:1], fvolt[1:2]] * 2, axis=1)
    fault = 10.0 * fv4 * (jnp.where(bus + g * BUS == fb4, 1.0, 0.0) * on4)

    all_boxes = remote(
        sbox.at[pl.ds(0, NGEN - 1)], rbox.at[pl.ds(0, NGEN - 1)], box_s, box_r, g, n
    )
    all_boxes.wait_recv()

    ids_in = rbox[:, 3, :]
    ids_t = ids_in.T
    id_lane = jnp.concatenate([ids_t[r : r + 1] for r in (0, 2, 4, 1, 3, 5)], axis=1)
    bus_hot = jnp.where((bus + 1).astype(F32) == id_lane, 1.0, 0.0).astype(BF16)
    summed = unpack(bus_hot, [rbox[:, j, :] for j in range(3)])
    inject = summed - fault
    first, second = inject[:128], inject[128:]
    i16 = row_iota((128, 128)) % 16
    second = jnp.where(i16 < 8, second, pltpu.roll(second, 96, 1))
    message = jnp.where(lane_iota((128, 128)) < 64, first, second).astype(BF16)
    smsg[...] = message.reshape(NNET, 16, 128)

    for k in (0, 1, 2):

        def send_msg(i, carry, k=k):
            peer = (n + i) % NNET
            gen = ((z + FAR[k]) % NZ) * NY + y
            remote(smsg.at[peer], rmsg.at[BACK[k], n], msg_s.at[k], msg_r.at[BACK[k]], gen, peer).start()
            return carry

        lax.fori_loop(0 if k else 1, NNET, send_msg, 0)
    rmsg[0, n] = smsg[n]

    def all_msgs(k):
        count = NNET if k else NNET - 1
        return remote(
            smsg.at[pl.ds(0, count)], rmsg.at[k, pl.ds(0, count)], msg_s.at[k], msg_r.at[k], g, n
        )

    slots = [(z + FAR[k]) % NZ for k in range(3)]
    for k in (0, 3, 1, 2):
        if k == 3:
            slots.append((z + FAR[3]) % NZ)
        else:
            slots += [(z + FAR[k] + NZ - d) % NZ for d in NEAR]
    origin = (0, 1, 2, 7)
    source = (0, 1, 2, 0, 0, 0, 0, 3, 1, 1, 1, 1, 2, 2, 2, 2)
    after = (3, 8, 12)

    def late(k):
        return pl.ds(EARLY[k], 3 - EARLY[k])

    def near_copy(k, way):
        ref = gath.at[slots[k], y, late(k)]
        gen = ((z + NEAR[way]) % NZ) * NY + y
        return remote(ref, ref, near_s.at[way, k], near_r.at[way, k], gen, n)

    def bundle_copy(k, way):
        ref = gath.at[slots[k], :, pl.ds(0, EARLY[k])]
        gen = ((z + NEAR[way]) % NZ) * NY + y
        return remote(ref, ref, bundle_s.at[way, k], bundle_r.at[way, k], gen, n)

    def far_copy():
        ref = gath.at[slots[0], y]
        gen = ((z + FAR[3]) % NZ) * NY + y
        return remote(ref, ref, far_s, far_r, gen, n)

    def early_copy(k, way):
        ref = gath.at[slots[origin[k]], y, pl.ds(0, EARLY[k])]
        gen = z * NY + (y + SIDE[way]) % NY
        return remote(ref, ref, early_s.at[way, k], early_r.at[way, k], gen, n)

    def side_copy(m, way):
        ref = gath.at[slots[m], y, late(source[m])]
        gen = z * NY + (y + SIDE[way]) % NY
        return remote(ref, ref, side_s.at[way, m], side_r.at[way, m], gen, n)

    def relay_copy(m, way):
        ref = gath.at[slots[m], (y + SIDE[1 - way]) % NY, 1 + way]
        gen = z * NY + (y + SIDE[way]) % NY
        return remote(ref, ref, relay_s.at[way, m], relay_r.at[way, m], gen, n)

    def send_sides(m):
        for way in range(2 if m in RELAY else 3):
            side_copy(m, way).start()

    def relay(m):
        for way in range(2):
            side_copy(m, way).wait_recv()
            relay_copy(m, way).start()

    def spread(k):
        for way in (2, 0, 1):
            early_copy(k, way).start()
        if k < 3:
            for way in (2, 3, 0, 1):
                near_copy(k, way).start()
        send_sides(origin[k])

    def assemble(k):
        all_msgs(k).wait_recv()
        tiles = [rmsg[k, m].astype(F32) for m in range(NNET)]
        for j in range(3):
            chunk = jnp.concatenate([t[:, SCN * j : SCN * (j + 1)] for t in tiles], axis=1)
            gath[slots[origin[k]], y, j] = chunk.astype(BF16)
        spread(k)
        if k == 0:
            far_copy().start()

    def bundle(k):
        for way in range(3):
            early_copy(k, way).wait_recv()
        if k < 3:
            for way in (2, 3, 0, 1):
                bundle_copy(k, way).start()

    def arrive(k, way):
        near_copy(k, way).wait_recv()
        send_sides(after[k] + way)

    assemble(0)
    turn(5)
    for way in range(2):
        arrive(0, way)
    bundle(0)
    for way in range(2, 4):
        arrive(0, way)
    relay(0)
    assemble(1)
    assemble(2)
    turn(6)
    far_copy().wait_recv()
    spread(3)
    for m in (3, 4, 5, 6):
        relay(m)
    bundle(1)
    bundle(2)
    for way in range(4):
        arrive(1, way)
    relay(7)
    for way in range(4):
        arrive(2, way)
    turn(7)
    bus_lane = lane_iota((NGEN, BUS)) + 1
    back_hot[...] = jnp.concatenate(
        [
            jnp.where(ids_in[:, r : r + 1].astype(jnp.int32) == bus_lane, 1.0, 0.0)
            for r in range(CAP)
        ],
        axis=0,
    ).astype(BF16)
    bundle(3)

    def product(group):
        total = None
        for m in group:
            part = jnp.dot(
                zt[slots[m]],
                gath[slots[m]].reshape(BUS, NNET * SCN),
                preferred_element_type=F32,
            )
            total = part if total is None else total + part
        return total

    groups = (range(0, 4), range(4, 8), range(8, 12), range(12, 16))
    for i, group in enumerate(groups):
        for m in group:
            for way in range(2 if m in RELAY else 3):
                (relay_copy if m in RELAY else side_copy)(m, way).wait_recv()
            for k in range(3):
                if after[k] <= m < after[k] + 4:
                    bundle_copy(k, m - after[k]).wait_recv()
        if i == 0:
            acc[...] = product(group)
        else:
            acc[...] += product(group)

    sib = n + 1 - 2 * c
    tiles = range(2 * BUS // TILE)

    def core_copy(q):
        return remote(vbuf.at[q, :, 1 - c], cbuf.at[q], core_s.at[q], core_r.at[q], g, sib)

    def x_all(q):
        return remote(
            wbuf.at[q, pl.ds(0, NX - 1)],
            xbuf.at[q, pl.ds(0, NX - 1)],
            x_s.at[q],
            x_r.at[q],
            g,
            n,
        )

    def finish(q):
        rows = slice(TILE * q, TILE * (q + 1))
        whole = acc[rows]
        vbuf[q] = whole.T.reshape(NX, NCORE, SCN, TILE)
        core_copy(q).start()

    def add_core(q):
        core_copy(q).wait_recv()
        wbuf[q] = vbuf[q, :, c] + cbuf[q]
        for d in (2, 1, 3):
            peer = (x + d) % NX
            remote(
                wbuf.at[q, peer], xbuf.at[q, x], x_s.at[q], x_r.at[q], g, peer * NCORE + c
            ).start()
        xbuf[q, x] = wbuf[q, x]

    for q in tiles:
        finish(q)
        if q:
            add_core(q - 1)
    add_core(tiles[-1])
    volts = []
    for q in tiles:
        x_all(q).wait_recv()
        volts.append((xbuf[q, 0] + xbuf[q, 1]) + (xbuf[q, 2] + xbuf[q, 3]))
    volts = jnp.concatenate(volts, axis=1)

    both = jnp.concatenate([volts[:, :BUS], volts[:, BUS:]], axis=0)
    for j, row in enumerate(pack(back_hot[...], both)):
        sback[:, j, :] = row

    def send_back(i, carry):
        peer = peer_at(i)
        remote(
            sback.at[peer, pl.ds(0, 3)], rback.at[g, pl.ds(0, 3)], back_s, back_r, peer, n
        ).start()
        return carry

    lax.fori_loop(0, NGEN - 1, send_back, 0)
    rback[g, 0:3] = sback[g, 0:3]

    all_boxes.wait_send()
    far_copy().wait_send()
    for k in range(4):
        for way in range(3):
            early_copy(k, way).wait_send()
        if k < 3:
            all_msgs(k).wait_send()
            for way in range(4):
                near_copy(k, way).wait_send()
                bundle_copy(k, way).wait_send()
    for m in range(NZ):
        for way in range(2 if m in RELAY else 3):
            side_copy(m, way).wait_send()
            if m in RELAY:
                relay_copy(m, way).wait_send()
    for q in tiles:
        core_copy(q).wait_send()
        x_all(q).wait_send()

    all_back = remote(
        sback.at[pl.ds(0, NGEN - 1), pl.ds(0, 3)],
        rback.at[pl.ds(0, NGEN - 1), pl.ds(0, 3)],
        back_s,
        back_r,
        g,
        n,
    )
    all_back.wait_recv()
    at_gen = unpack(slot_hot[...], [rback[:, j, :] for j in range(3)]).T
    v_re, v_im = at_gen[:SCN], at_gen[SCN : 2 * SCN]

    sin_d, cos_d, emf_re, emf_im = keep[0], keep[1], keep[2], keep[3]
    omega, eq_t, eq_s, ed_s, efd = state[1], state[2], state[3], state[4], state[5]
    par = [params[k : k + 1, :] for k in range(13)]
    gen_re = (emf_im - v_im) / sub_x
    gen_im = (v_re - emf_re) / sub_x
    cur_d = gen_re * sin_d - gen_im * cos_d
    cur_q = gen_re * cos_d + gen_im * sin_d
    power = ed_s * cur_d + eq_s * cur_q
    term = jnp.sqrt(v_re * v_re + v_im * v_im + 0.01)
    out[0] = omega * active
    out[1] = (par[12] - power - par[1] * omega) / (2.0 * par[0]) * active
    out[2] = (efd - eq_t - (par[5] - par[6]) * cur_d) / par[2] * active
    out[3] = (eq_t - eq_s - (par[6] - sub_x) * cur_d) / par[3] * active
    out[4] = ((par[8] - sub_x) * cur_q - ed_s) / par[4] * active
    out[5] = (par[9] * (par[11] - term) - efd) / par[10] * active

    all_back.wait_send()


def body(state, params, gen_count, gen_block, gen_local, impedance, fault_bus, cleared, fault_volt):
    dma = pltpu.SemaphoreType.DMA
    inputs = (
        state,
        params,
        gen_count,
        gen_block.reshape(1, SLOTS),
        gen_local.reshape(1, SLOTS),
        impedance.reshape(2, NZ // 2, BUS, 2 * BUS),
        fault_bus.reshape(1, SCN),
        cleared.reshape(1, SCN),
        fault_volt,
    )
    return pl.pallas_call(
        kernel,
        out_shape=jax.ShapeDtypeStruct(state.shape, F32),
        in_specs=[pl.BlockSpec(memory_space=pltpu.HBM)] * len(inputs),
        out_specs=pl.BlockSpec(memory_space=pltpu.VMEM),
        scratch_shapes=[
            (pltpu.SMEM if v.ndim == 1 else pltpu.VMEM)(v.shape, v.dtype) for v in inputs
        ]
        + [
            pltpu.VMEM((NZ, 2 * BUS, BUS), BF16),
            pltpu.VMEM((NZ, NY, 3, 16, NNET * SCN), BF16),
            pltpu.VMEM((NGEN, 4, 128), F32),
            pltpu.VMEM((NGEN, 4, 128), F32),
            pltpu.VMEM((NNET, 16, 128), BF16),
            pltpu.VMEM((3, NNET, 16, 128), BF16),
            pltpu.VMEM((2 * BUS // TILE, NX, NCORE, SCN, TILE), F32),
            pltpu.VMEM((2 * BUS // TILE, NX, SCN, TILE), F32),
            pltpu.VMEM((2 * BUS // TILE, NX, SCN, TILE), F32),
            pltpu.VMEM((2 * BUS // TILE, NX, SCN, TILE), F32),
            pltpu.VMEM((NGEN, 4, 128), F32),
            pltpu.VMEM((NGEN, 4, 128), F32),
            pltpu.VMEM((4, SCN, SLOTS), F32),
            pltpu.VMEM((CAP * NGEN, BUS), BF16),
            pltpu.VMEM((SLOTS, CAP * NGEN), BF16),
            pltpu.VMEM((2 * BUS, NNET * SCN), F32),
            dma((9,)),
            dma,
            dma,
            dma((3,)),
            dma((3,)),
            dma,
            dma,
            dma((4, 3)),
            dma((4, 3)),
            dma((4, 3)),
            dma((4, 3)),
            dma((3, 4)),
            dma((3, 4)),
            dma((3, NZ)),
            dma((3, NZ)),
            dma((2, NZ)),
            dma((2, NZ)),
            dma((2 * BUS // TILE,)),
            dma((2 * BUS // TILE,)),
            dma((2 * BUS // TILE,)),
            dma((2 * BUS // TILE,)),
            dma,
            dma,
        ],
        compiler_params=pltpu.CompilerParams(
            collective_id=0, has_side_effects=True, vmem_limit_bytes=64 * 1024 * 1024 - 65536
        ),
    )(*inputs)


def solution(mesh):
    in_specs = (
        P(None, "net", "gen"),
        P(None, "gen"),
        P("gen"),
        P("gen", None),
        P("gen"),
        P(None, "net", "gen"),
        P("net"),
        P("net"),
        P(None, "net"),
    )
    return jax.shard_map(
        body, mesh=mesh, in_specs=in_specs, out_specs=P(None, "net", "gen"), check_vma=False
    )
```
